32 devices in a mesh: row: 8 (over y, x, core), col: 4 (over z).
Axes of the slice: x: 2, y: 2, z: 4, core: 2. Of those that a mesh axis runs over, the one named last changes fastest.
Arguments:
- factor_rows: bfloat16 [2, 1024, 16384], P(None, None, ('row', 'col')), may hold values from -0.09375 to 0.09375
- solved: bfloat16 [64, 16384], P(None, ('row', 'col')), may hold values from -6 to 6
- inverses: bfloat16 [2, 1024, 1024], P(None, 'row', 'col'), as said below
- link_tile: bfloat16 [1024, 1024], P('col', 'row'), may hold values from -0.1875 to 0.1875
- right_side: float32 [2, 1024, 64], P(None, 'col'), may hold values from -6 to 6
Outputs:
- back_solved: float32 [2, 1024, 64], P(None, 'col')
- remaining: float32 [64, 16384], P(None, ('row', 'col'))
The draws below stay inside these ranges and needn't reach their ends.
Inputs may be any that keep to these rules, and one draw needn't show every extreme that they name: `inverses`: each of the two blocks is lower triangular with a positive diagonal.
All inputs are finite; a program needn't handle non-finite values.
Results may differ from the reference program's by a relative error of at most 0.015.
Values may be sent and summed in bfloat16 or wider, within the bound.
No kernel may reach another device: no remote copies, remote signals or barrier semaphores. Data moves between devices by JAX's collectives and lax.ppermute only.
A program may use at most 64 MiB of HBM per device.

```python
import math
import jax
import jax.numpy as jnp
from jax import lax

BS = 1024
NRHS = 64
COLUMNS = 16384


def draw_inverses(key, part):
    first_key = jax.random.fold_in(key, 11)
    second_key = jax.random.fold_in(key, 12)
    lower_vals = jax.random.normal(first_key, (2, BS, BS), jnp.float32)
    lower_vals = lower_vals * (0.5 / math.sqrt(BS))
    diagonal_vals = 0.6 + 0.8 * jax.random.uniform(second_key, (2, BS, BS), jnp.float32)
    places = jnp.arange(BS)
    below = places[:, None] > places[None, :]
    on_diag = places[:, None] == places[None, :]
    matrix = jnp.where(below[None], lower_vals, 0.0) + jnp.where(on_diag[None], diagonal_vals, 0.0)
    return matrix.astype(jnp.bfloat16)


def spiked(drawn, own_key, source, target, blocks, factor):
    def block_of(position):
        return (jnp.arange(drawn.shape[position]) // (drawn.shape[position] // blocks)).reshape((-1,) + (1,) * (drawn.ndim - 1 - position))

    one_side = jax.random.permutation(own_key, blocks)[block_of(target)]
    second = (block_of(target) + blocks // 2) % blocks
    return jnp.where((block_of(source) == one_side) | (block_of(source) == second), factor * drawn, drawn)


def steps_of(key, dims, pieces, low, high):
    gain = 1.0
    for position, blocks in pieces:
        heights = jax.random.uniform(jax.random.fold_in(jax.random.fold_in(key, 6), position), (blocks,), jnp.float32, low / len(pieces), high / len(pieces))
        gain = gain * jnp.repeat(jnp.exp(heights), dims[position] // blocks).reshape((-1,) + (1,) * (len(dims) - 1 - position))
    return gain


def noise(rng, shape, spread, bound, shards=(), kind=jnp.bfloat16):
    result = jax.random.normal(rng, shape, jnp.float32) * spread
    if len(shards) > 0:
        result = steps_of(rng, shape, shards, -0.22, 0.18) * result
    return jnp.clip(result, min=-bound, max=bound).astype(kind)


def gaussian_with(key, dims, deviation, most, cuts, heavy, held_as=jnp.bfloat16):
    entries = deviation * jax.random.normal(key, dims, jnp.float32)
    if cuts:
        entries = entries * steps_of(key, dims, cuts, -0.22, 0.18)
    return jnp.clip(spiked(entries, jax.random.fold_in(key, 3), *heavy), -most, most).astype(held_as)


def setup_inputs(seed: int = 0) -> dict:
    key_list = jax.random.split(jax.random.key(seed), 6)
    factor_rows = gaussian_with(key_list[0], (2, BS, COLUMNS), COLUMNS ** -0.5, 0.09375, ((2, 32),), (2, 1, 32, 2.75))
    solved = noise(key_list[1], (NRHS, COLUMNS), 1.0, 6.0, ((1, 32),))
    inverses = draw_inverses(jax.random.fold_in(key_list[5], 71), 0)
    link_tile = noise(key_list[3], (BS, BS), BS ** -0.5, 0.1875, ((0, 4), (1, 8)))
    right_side = noise(key_list[4], (2, BS, NRHS), 1.0, 6.0, ((1, 4),), jnp.float32)
    return {"factor_rows": factor_rows, "solved": solved, "inverses": inverses, "link_tile": link_tile, "right_side": right_side}


def reference(factor_rows, solved, inverses, link_tile, right_side):
    count = COLUMNS // BS

    def add_block(index, carried):
        start = (index * BS).astype(jnp.int32)
        columns = lax.dynamic_slice_in_dim(factor_rows, start, BS, 2)
        targets = lax.dynamic_slice_in_dim(solved, start, BS, 1)
        upper = jnp.dot(columns[0], targets.T, preferred_element_type=jnp.float32)
        lower = jnp.dot(columns[1], targets.T, preferred_element_type=jnp.float32)
        return carried + jnp.stack([upper, lower])

    panel_sum = lax.fori_loop(jnp.int32(0), jnp.int32(count), add_block, jnp.zeros((2, BS, NRHS), jnp.float32))
    residue_first = (right_side[0] - panel_sum[0]).astype(jnp.bfloat16)
    first_solved = jnp.dot(inverses[0], residue_first, preferred_element_type=jnp.float32).astype(jnp.bfloat16)
    link_term = jnp.dot(link_tile, first_solved, preferred_element_type=jnp.float32)
    residue_last = (right_side[1] - panel_sum[1] - link_term).astype(jnp.bfloat16)
    last_solved = jnp.dot(inverses[1], residue_last, preferred_element_type=jnp.float32).astype(jnp.bfloat16)
    last_out = jnp.dot(inverses[1].T, last_solved, preferred_element_type=jnp.float32)
    last_short = last_out.astype(jnp.bfloat16)
    back_term = jnp.dot(link_tile.T, last_short, preferred_element_type=jnp.float32)
    carry = (first_solved.astype(jnp.float32) - back_term).astype(jnp.bfloat16)
    first_out = jnp.dot(inverses[0].T, carry, preferred_element_type=jnp.float32)
    first_short = first_out.astype(jnp.bfloat16)

    def update_block(index):
        start = (index * BS).astype(jnp.int32)
        columns = lax.dynamic_slice_in_dim(factor_rows, start, BS, 2)
        targets = lax.dynamic_slice_in_dim(solved, start, BS, 1).astype(jnp.float32)
        upper = jnp.dot(first_short.T, columns[0], preferred_element_type=jnp.float32)
        lower = jnp.dot(last_short.T, columns[1], preferred_element_type=jnp.float32)
        return targets - upper - lower

    blocks = lax.map(update_block, jnp.arange(count, dtype=jnp.int32))
    remaining = jnp.transpose(blocks, (1, 0, 2)).reshape(NRHS, COLUMNS)
    back_solved = jnp.stack([first_out, last_out])
    return back_solved, remaining
```

```python
import jax
import jax.numpy as jnp
from jax import lax
from jax.sharding import PartitionSpec as P

BF = jnp.bfloat16
F32 = jnp.float32


def dot(left, right, contract):
    return lax.dot_general(left, right, ((contract[0], contract[1]), ((), ())), preferred_element_type=F32)


def build(R, C):
    def exchange(value, axes):
        return lax.all_to_all(value, axes, 0, 0, tiled=False)

    def xor_row(value, step):
        return lax.ppermute(value, "row", [(i, i ^ step) for i in range(R)])

    def sum_over_col(part):
        sent = jnp.broadcast_to(part.astype(BF)[None], (C,) + part.shape)
        return jnp.sum(exchange(sent, "col").astype(F32), axis=0)

    def shards(factor_rows, solved, inverses, link_tile, right_side):
        nrhs = solved.shape[0]
        group = nrhs // R
        rows = right_side.shape[1]
        order = rows * C
        own = jnp.concatenate([inverses, link_tile.T[None]], axis=0)
        near = [own] + [xor_row(own, step) for step in range(2, R, 2)]
        near = jnp.stack(near, axis=1)
        mate = xor_row(near, 1)
        weights = jnp.concatenate([near, mate], axis=1).reshape(3, order, rows)
        first_tile, last_tile, link_back = weights[0], weights[1], weights[2]

        part = jnp.einsum("nc,kic->nki", solved, factor_rows, preferred_element_type=F32).astype(BF)
        part = part.reshape(R, group, 2, C, rows).transpose(0, 3, 2, 1, 4).reshape(R * C, 2 * group, rows)
        panel = jnp.sum(exchange(part, ("row", "col")).astype(F32), axis=0).reshape(2, group, rows)
        mine = lax.dynamic_slice_in_dim(right_side, lax.axis_index("row") * group, group, 2)
        residue = mine.transpose(0, 2, 1) - panel

        first_solved = sum_over_col(dot(residue[0].astype(BF), first_tile, ((1,), (1,)))).astype(BF)
        link_term = dot(first_solved, link_back, ((1,), (0,)))
        residue_last = (residue[1] - link_term).astype(BF)
        last_solved = sum_over_col(dot(residue_last, last_tile, ((1,), (1,)))).astype(BF)
        last_short = dot(last_solved, last_tile, ((1,), (0,))).astype(BF)
        back_term = sum_over_col(dot(last_short, link_back, ((1,), (1,))))
        carry = (first_solved.astype(F32) - back_term).astype(BF)
        first_short = dot(carry, first_tile, ((1,), (0,))).astype(BF)

        both = jnp.concatenate([first_short, last_short], axis=0)
        sent = jnp.broadcast_to(both[None], (R * C,) + both.shape)
        whole = exchange(sent, ("row", "col")).reshape(R, C, 2, group, rows)
        whole = whole.transpose(2, 0, 3, 1, 4).reshape(2, nrhs, order)
        update = jnp.einsum("kni,kic->nc", whole, factor_rows, preferred_element_type=F32)
        remaining = solved.astype(F32) - update
        here = lax.dynamic_slice_in_dim(whole, lax.axis_index("col") * rows, rows, 2)
        return (here.astype(F32).transpose(0, 2, 1), remaining)

    return shards


def solution(mesh):
    placed = (
        P(None, None, ("row", "col")),
        P(None, ("row", "col")),
        P(None, "row", "col"),
        P("col", "row"),
        P(None, "col", None),
    )
    return jax.shard_map(
        build(mesh.shape["row"], mesh.shape["col"]),
        mesh=mesh,
        in_specs=placed,
        out_specs=(P(None, "col", None), P(None, ("row", "col"))),
        check_vma=False,
    )
```

```python
import functools

import jax
import jax.numpy as jnp
from jax import lax
from jax.experimental import pallas as pl
from jax.experimental.pallas import tpu as pltpu
from jax.sharding import PartitionSpec as P

BF = jnp.bfloat16
F32 = jnp.float32
PARAMS = pltpu.CompilerParams(vmem_limit_bytes=40 * 2**20)


def dot(left, right, contract):
    return lax.dot_general(left, right, ((contract[0], contract[1]), ((), ())), preferred_element_type=F32)


def plain(left, right):
    return dot(left, right, ((1,), (0,)))


def flipped(left, right):
    return dot(left, right, ((1,), (1,)))


def exchange(value, axes):
    return lax.all_to_all(value, axes, 0, 0, tiled=False)


def generic(R, C):
    def xor_row(value, step):
        return lax.ppermute(value, "row", [(i, i ^ step) for i in range(R)])

    def sum_over_col(part):
        sent = jnp.broadcast_to(part.astype(BF)[None], (C,) + part.shape)
        return jnp.sum(exchange(sent, "col").astype(F32), axis=0)

    def shards(factor_rows, solved, inverses, link_tile, right_side):
        nrhs = solved.shape[0]
        group = nrhs // R
        rows = right_side.shape[1]
        order = rows * C
        own = jnp.concatenate([inverses, link_tile.T[None]], axis=0)
        near = [own] + [xor_row(own, step) for step in range(2, R, 2)]
        near = jnp.stack(near, axis=1)
        mate = xor_row(near, 1)
        weights = jnp.concatenate([near, mate], axis=1).reshape(3, order, rows)
        first_tile, last_tile, link_back = weights[0], weights[1], weights[2]

        part = jnp.einsum("nc,kic->nki", solved, factor_rows, preferred_element_type=F32).astype(BF)
        part = part.reshape(R, group, 2, C, rows).transpose(0, 3, 2, 1, 4).reshape(R * C, 2 * group, rows)
        panel = jnp.sum(exchange(part, ("row", "col")).astype(F32), axis=0).reshape(2, group, rows)
        mine = lax.dynamic_slice_in_dim(right_side, lax.axis_index("row") * group, group, 2)
        residue = mine.transpose(0, 2, 1) - panel

        first_solved = sum_over_col(flipped(residue[0].astype(BF), first_tile)).astype(BF)
        residue_last = (residue[1] - plain(first_solved, link_back)).astype(BF)
        last_solved = sum_over_col(flipped(residue_last, last_tile)).astype(BF)
        last_short = plain(last_solved, last_tile).astype(BF)
        back_term = sum_over_col(flipped(last_short, link_back))
        carry = (first_solved.astype(F32) - back_term).astype(BF)
        first_short = plain(carry, first_tile).astype(BF)

        both = jnp.concatenate([first_short, last_short], axis=0)
        sent = jnp.broadcast_to(both[None], (R * C,) + both.shape)
        return finish(factor_rows, solved, exchange(sent, ("row", "col")), R, C)

    return shards


def finish(factor_rows, solved, arrived, R, C):
    nrhs = solved.shape[0]
    group, rows = nrhs // R, arrived.shape[2]
    whole = arrived.reshape(R, C, 2, group, rows)
    whole = whole.transpose(2, 0, 3, 1, 4).reshape(2, nrhs, rows * C)
    update = jnp.einsum("kni,kic->nc", whole, factor_rows, preferred_element_type=F32)
    remaining = solved.astype(F32) - update
    here = lax.dynamic_slice_in_dim(whole, lax.axis_index("col") * rows, rows, 2)
    return (here.astype(F32).transpose(0, 2, 1), remaining)


def pack_kernel(inv_ref, link_ref, own_ref, far_ref):
    own_ref[0] = inv_ref[0]
    own_ref[1] = inv_ref[1]
    far_ref[0] = inv_ref[1]
    turned = link_ref[...].T
    own_ref[2] = turned
    far_ref[1] = turned


def panel_kernel(solved_ref, factor_ref, part_ref):
    R, _, double, rows = part_ref.shape
    group = double // 2
    value = solved_ref[...]
    upper = flipped(value, factor_ref[0]).reshape(R, group, rows)
    lower = flipped(value, factor_ref[1]).reshape(R, group, rows)
    part_ref[:, 0] = jnp.concatenate([upper, lower], axis=1).astype(BF)


def stack_kernel(*refs):
    for i, ref in enumerate(refs[:-1]):
        refs[-1][i] = ref[...]


def first_kernel(count, near, panel_ref, side_ref, *refs):
    tiles, sent_ref = refs[:near], refs[near]
    group = side_ref.shape[0] // 2
    total = panel_ref[0].astype(F32)
    for i in range(1, panel_ref.shape[0]):
        total += panel_ref[i].astype(F32)
    residue = side_ref[...] - total
    first = residue[:group].astype(BF)
    last = residue[group:]
    outs = [flipped(first, tile[0]) for tile in tiles]
    half = near // 2
    top = jnp.concatenate(outs[:half] + [last[:, : last.shape[1] // 2]], axis=1)
    low = jnp.concatenate(outs[half:] + [last[:, last.shape[1] // 2 :]], axis=1)
    both = jnp.concatenate([top, low], axis=0).astype(BF)
    for i in range(count):
        sent_ref[i] = both


def chain_kernel(near, C, arrived_ref, *refs):
    tiles, others, sent_ref = refs[:near], refs[near : 2 * near], refs[2 * near]
    here = lax.axis_index("col")
    group = arrived_ref.shape[1] // 2
    size = tiles[0].shape[1]
    half = near // 2
    wide = half * size
    total = arrived_ref[0, :, :wide].astype(F32)
    for i in range(1, C):
        total += arrived_ref[i, :, :wide].astype(F32)
    total = total.astype(BF)
    first = [total[(s // half) * group : (s // half + 1) * group, (s % half) * size : (s % half + 1) * size] for s in range(near)]

    def last_tile(s, z):
        return tiles[s][1] if z == 0 else others[s][z - 1, 0]

    def link_back(s, z):
        return tiles[s][2] if z == 0 else others[s][z - 1, 1]

    turn = []
    for z in range(C):
        raw = arrived_ref[here ^ z, :, wide:].astype(F32)
        value = jnp.concatenate([raw[:group], raw[group:]], axis=1)
        for s in range(near):
            value -= plain(first[s], link_back(s, z))
        turn.append(value.astype(BF))
    last = []
    for s in range(near):
        value = flipped(turn[0], last_tile(s, 0))
        for z in range(1, C):
            value += flipped(turn[z], last_tile(s, z))
        last.append(value.astype(BF))
    short = []
    for z in range(C):
        value = plain(last[0], last_tile(0, z))
        for s in range(1, near):
            value += plain(last[s], last_tile(s, z))
        short.append(value.astype(BF))
    first_out = None
    for s in range(near):
        carry = first[s].astype(F32)
        for z in range(C):
            carry -= flipped(short[z], link_back(s, z))
        value = plain(carry.astype(BF), tiles[s][0])
        first_out = value if first_out is None else first_out + value
    both = jnp.concatenate([first_out.astype(BF), short[0]], axis=0)
    for i in range(sent_ref.shape[0]):
        sent_ref[i] = both


def tiled(R, C):
    def xor_row(value, step):
        return lax.ppermute(value, "row", [(i, i ^ step) for i in range(R)])

    def xor_col(value, step):
        return lax.ppermute(value, "col", [(i, i ^ step) for i in range(C)])

    def shards(factor_rows, solved, inverses, link_tile, right_side):
        nrhs, width = solved.shape
        group = nrhs // R
        rows = right_side.shape[1]
        size = inverses.shape[1]
        order = rows * C
        own, far = pl.pallas_call(
            pack_kernel,
            out_shape=(
                jax.ShapeDtypeStruct((3, size, rows), BF),
                jax.ShapeDtypeStruct((2, size, rows), BF),
            ),
            compiler_params=PARAMS,
        )(inverses, link_tile)
        fars = [xor_col(far, step) for step in range(1, C)]
        evens = [own] + [xor_row(own, step) for step in range(2, R, 2)]
        tiles = [block for even in evens for block in (even, xor_row(even, 1))]

        part = pl.pallas_call(
            panel_kernel,
            grid=(C,),
            in_specs=[
                pl.BlockSpec((nrhs, width), lambda c: (0, 0)),
                pl.BlockSpec((2, rows, width), lambda c: (0, c, 0)),
            ],
            out_specs=pl.BlockSpec((R, 1, 2 * group, rows), lambda c: (0, c, 0, 0)),
            out_shape=jax.ShapeDtypeStruct((R, C, 2 * group, rows), BF),
            compiler_params=PARAMS,
        )(solved, factor_rows)
        mine = lax.dynamic_slice_in_dim(right_side, lax.axis_index("row") * group, group, 2)
        mine = mine.transpose(0, 2, 1).reshape(2 * group, rows)
        panel = exchange(part.reshape(R * C, 2 * group, rows), ("row", "col"))

        stack = pl.pallas_call(
            stack_kernel,
            out_shape=jax.ShapeDtypeStruct((C - 1, 2, size, rows), BF),
            compiler_params=PARAMS,
        )(*fars)
        evens = [stack] + [xor_row(stack, step) for step in range(2, R, 2)]
        others = [block for even in evens for block in (even, xor_row(even, 1))]

        wide = (order + rows) // 2
        only_first = pl.BlockSpec((1, size, rows), lambda i: (0, 0, 0))
        sent = pl.pallas_call(
            functools.partial(first_kernel, C, R),
            grid=(1,),
            in_specs=[
                pl.BlockSpec(panel.shape, lambda i: (0, 0, 0)),
                pl.BlockSpec(mine.shape, lambda i: (0, 0)),
            ]
            + [only_first] * R,
            out_specs=pl.BlockSpec((C, 2 * group, wide), lambda i: (0, 0, 0)),
            out_shape=jax.ShapeDtypeStruct((C, 2 * group, wide), BF),
            compiler_params=PARAMS,
        )(panel, mine, *tiles)
        arrived = exchange(sent, "col")
        sent = pl.pallas_call(
            functools.partial(chain_kernel, R, C),
            out_shape=jax.ShapeDtypeStruct((R * C, 2 * group, rows), BF),
            compiler_params=PARAMS,
        )(arrived, *tiles, *others)
        return finish(factor_rows, solved, exchange(sent, ("row", "col")), R, C)

    return shards


def solution(mesh):
    R, C = mesh.shape["row"], mesh.shape["col"]

    def shards(factor_rows, solved, inverses, link_tile, right_side):
        group = solved.shape[0] // R
        aligned = group % 8 == 0 and inverses.shape[1] % 128 == 0 and inverses.shape[2] % 256 == 0
        build = tiled if aligned else generic
        return build(R, C)(factor_rows, solved, inverses, link_tile, right_side)

    placed = (
        P(None, None, ("row", "col")),
        P(None, ("row", "col")),
        P(None, "row", "col"),
        P("col", "row"),
        P(None, "col", None),
    )
    return jax.shard_map(
        shards,
        mesh=mesh,
        in_specs=placed,
        out_specs=(P(None, "col", None), P(None, ("row", "col"))),
        check_vma=False,
    )
```

```python
import functools

import jax
import jax.numpy as jnp
from jax import lax
from jax.experimental import pallas as pl
from jax.experimental.pallas import tpu as pltpu
from jax.sharding import PartitionSpec as P

BF = jnp.bfloat16
F32 = jnp.float32
PARAMS = pltpu.CompilerParams(vmem_limit_bytes=12 * 2**20)
WIDE = pltpu.CompilerParams(vmem_limit_bytes=62 * 2**20)


def dot(left, right, contract):
    return lax.dot_general(left, right, ((contract[0], contract[1]), ((), ())), preferred_element_type=F32)


def plain(left, right):
    return dot(left, right, ((1,), (0,)))


def flipped(left, right):
    return dot(left, right, ((1,), (1,)))


def exchange(value, axes):
    return lax.all_to_all(value, axes, 0, 0, tiled=False)


def generic(R, C):
    def xor_row(value, step):
        return lax.ppermute(value, "row", [(i, i ^ step) for i in range(R)])

    def sum_over_col(part):
        sent = jnp.broadcast_to(part.astype(BF)[None], (C,) + part.shape)
        return jnp.sum(exchange(sent, "col").astype(F32), axis=0)

    def shards(factor_rows, solved, inverses, link_tile, right_side):
        nrhs = solved.shape[0]
        group = nrhs // R
        rows = right_side.shape[1]
        order = rows * C
        own = jnp.concatenate([inverses, link_tile.T[None]], axis=0)
        near = [own] + [xor_row(own, step) for step in range(2, R, 2)]
        near = jnp.stack(near, axis=1)
        mate = xor_row(near, 1)
        weights = jnp.concatenate([near, mate], axis=1).reshape(3, order, rows)
        first_tile, last_tile, link_back = weights[0], weights[1], weights[2]

        part = jnp.einsum("nc,kic->nki", solved, factor_rows, preferred_element_type=F32).astype(BF)
        part = part.reshape(R, group, 2, C, rows).transpose(0, 3, 2, 1, 4).reshape(R * C, 2 * group, rows)
        panel = jnp.sum(exchange(part, ("row", "col")).astype(F32), axis=0).reshape(2, group, rows)
        mine = lax.dynamic_slice_in_dim(right_side, lax.axis_index("row") * group, group, 2)
        residue = mine.transpose(0, 2, 1) - panel

        first_solved = sum_over_col(flipped(residue[0].astype(BF), first_tile)).astype(BF)
        residue_last = (residue[1] - plain(first_solved, link_back)).astype(BF)
        last_solved = sum_over_col(flipped(residue_last, last_tile)).astype(BF)
        last_short = plain(last_solved, last_tile).astype(BF)
        back_term = sum_over_col(flipped(last_short, link_back))
        carry = (first_solved.astype(F32) - back_term).astype(BF)
        first_short = plain(carry, first_tile).astype(BF)

        both = jnp.concatenate([first_short, last_short], axis=0)
        sent = jnp.broadcast_to(both[None], (R * C,) + both.shape)
        whole = exchange(sent, ("row", "col")).reshape(R, C, 2, group, rows)
        whole = whole.transpose(2, 0, 3, 1, 4).reshape(2, nrhs, order)
        return finish(factor_rows, solved, (whole[0], whole[1]), rows)

    return shards


def finish(factor_rows, solved, both, rows):
    update = plain(both[0], factor_rows[0]) + plain(both[1], factor_rows[1])
    remaining = solved.astype(F32) - update
    here = [lax.dynamic_slice_in_dim(one, lax.axis_index("col") * rows, rows, 1) for one in both]
    return (jnp.stack([one.astype(F32).T for one in here]), remaining)


def fold(value):
    half = value.shape[-1] // 2
    return jnp.concatenate([value[..., :half], value[..., half:]], axis=-2)


def unfold(value):
    half = value.shape[-2] // 2
    return jnp.concatenate([value[..., :half, :], value[..., half:, :]], axis=-1)


def pack_kernel(inv_ref, link_ref, first_ref, pair_ref):
    first_ref[0] = inv_ref[0]
    pair_ref[0] = inv_ref[1]
    pair_ref[1] = link_ref[...].T


def stack_kernel(own_ref, far_ref, both_ref):
    both_ref[:2] = own_ref[...]
    both_ref[2:] = far_ref[...]


def order_kernel(value_ref, part_ref):
    R, C, double, rows = part_ref.shape
    for c in range(C):
        halves = [value_ref[k, :, c * rows : (c + 1) * rows].astype(F32).reshape(R, double // 2, rows) for k in range(2)]
        part_ref[:, c] = jnp.concatenate(halves, axis=1).astype(BF)


def closing_kernel(C, solved_ref, factor_ref, whole_ref, remaining_ref, back_ref):
    group, rows = whole_ref.shape[1] // 2, whole_ref.shape[2]
    nrhs = solved_ref.shape[0]
    R = nrhs // group
    here = lax.axis_index("col")

    def columns(k, c):
        return jnp.concatenate([whole_ref[r * C + c, k * group : (k + 1) * group].astype(F32) for r in range(R)], axis=0)

    update = None
    for k in range(2):
        back_ref[k] = columns(k, here)
        for c in range(C):
            term = plain(columns(k, c).astype(BF), factor_ref[k, c * rows : (c + 1) * rows])
            update = term if update is None else update + term
    remaining_ref[...] = solved_ref[...].astype(F32) - update


def across(value, tiles):
    return jnp.concatenate([flipped(value, tile[0]) for tile in tiles], axis=1)


def along(value, tiles):
    size = tiles[0].shape[1]
    total = None
    for s, tile in enumerate(tiles):
        term = plain(value[:, s * size : (s + 1) * size], tile[0])
        total = term if total is None else total + term
    return total


def first_kernel(side_ref, panel_ref, *refs):
    tiles, sent_ref = refs[:-1], refs[-1]
    group = side_ref.shape[0] // 2
    total = panel_ref[0].astype(F32)
    for i in range(1, panel_ref.shape[0]):
        total += panel_ref[i].astype(F32)
    residue = side_ref[...] - total
    solved = across(residue[:group].astype(BF), tiles)
    sent_ref[...] = jnp.concatenate([fold(solved), fold(residue[group:])], axis=1).astype(BF)


def pair_sum(own_ref, other_ref):
    return unfold(own_ref[...].astype(F32) + other_ref[...].astype(F32))


def link_kernel(near, own_ref, other_ref, side_ref, *refs):
    links, last_tiles = refs[: 2 * near], refs[2 * near : 4 * near]
    sent_ref, first_ref = refs[4 * near :]
    first = pair_sum(own_ref, other_ref).astype(BF)
    first_ref[...] = first
    total = None
    for j in range(2):
        residue = unfold(side_ref[j].astype(F32)) - along(first, links[j * near : (j + 1) * near])
        term = across(residue.astype(BF), last_tiles[j * near : (j + 1) * near])
        total = term if total is None else total + term
    sent_ref[...] = fold(total).astype(BF)


def turn_kernel(near, own_ref, other_ref, *refs):
    last_tiles, links = refs[: 2 * near], refs[2 * near : 4 * near]
    sent_ref, short_ref = refs[4 * near :]
    last = pair_sum(own_ref, other_ref).astype(BF)
    total = None
    for j in range(2):
        short = along(last, last_tiles[j * near : (j + 1) * near]).astype(BF)
        if j == 0:
            short_ref[...] = short
        term = across(short, links[j * near : (j + 1) * near])
        total = term if total is None else total + term
    sent_ref[...] = fold(total).astype(BF)


def last_kernel(first_ref, short_ref, own_ref, other_ref, *refs):
    tiles, sent_ref = refs[:-1], refs[-1]
    carry = (first_ref[...].astype(F32) - pair_sum(own_ref, other_ref)).astype(BF)
    both = jnp.concatenate([along(carry, tiles), short_ref[...].astype(F32)], axis=0).astype(BF)
    for i in range(sent_ref.shape[0]):
        sent_ref[i] = both


def whole_spec(shape):
    return pl.BlockSpec(shape, lambda i: (0,) * len(shape))


def call(kernel, operands, tiles, shapes, params=PARAMS):
    def tile_spec(array, which):
        return pl.BlockSpec((1,) + array.shape[1:], lambda i: (which, 0, 0))

    return pl.pallas_call(
        kernel,
        grid=(1,),
        in_specs=[whole_spec(one.shape) for one in operands] + [tile_spec(*tile) for tile in tiles],
        out_specs=[whole_spec(shape) for shape in shapes],
        out_shape=[jax.ShapeDtypeStruct(shape, BF) for shape in shapes],
        compiler_params=params,
    )(*operands, *[tile[0] for tile in tiles])


def tiled(R, C):
    def xor_row(value, step):
        return lax.ppermute(value, "row", [(i, i ^ step) for i in range(R)])

    def xor_col(value, step):
        return lax.ppermute(value, "col", [(i, i ^ step) for i in range(C)])

    def in_plane(value):
        return [value] + [xor_row(value, step) for step in range(2, R, 2)]

    def with_mates(evens):
        return [block for even in evens for block in (even, xor_row(even, 1))]

    def shards(factor_rows, solved, inverses, link_tile, right_side):
        nrhs = solved.shape[0]
        group = nrhs // R
        rows = right_side.shape[1]
        size = inverses.shape[1]
        order = rows * C
        cut = (2 * group, rows)

        first_own, pair = call(pack_kernel, [inverses, link_tile], [], [(1, size, rows), (2, size, rows)], WIDE)
        held = solved
        part = jnp.einsum("nc,kic->nki", held, factor_rows, preferred_element_type=F32).astype(BF)
        part = part.reshape(R, group, 2, C, rows).transpose(0, 3, 2, 1, 4)
        far = xor_col(pair, 1)
        first_in = first_own
        evens = in_plane(first_in)
        part, *_ = lax.optimization_barrier((part, far, *evens))
        panel = exchange(part.reshape((R * C,) + cut), ("row", "col"))
        mine = lax.dynamic_slice_in_dim(right_side, lax.axis_index("row") * group, group, 2)
        mine = mine.transpose(0, 2, 1).reshape(cut)

        first_tiles = [(tile, 0) for tile in with_mates(evens)]
        own_pair = pair
        (both,) = call(stack_kernel, [own_pair, far], [], [(4, size, rows)])
        wide = order // 2
        summed = (2 * group, wide)
        (sent,) = call(first_kernel, [mine, panel], first_tiles, [(2 * group, wide + rows // 2)])
        evens = in_plane(both)
        arrived = xor_col(sent, 1)
        mates = []
        spare = evens[0]
        spare, *_ = lax.optimization_barrier((spare, arrived))
        mates.append(xor_row(spare, 1))
        spare = evens[1]
        spare, *_ = lax.optimization_barrier((spare, arrived))
        mates.append(xor_row(spare, 1))
        spare = evens[2]
        spare, *_ = lax.optimization_barrier((spare, arrived))
        mates.append(xor_row(spare, 1))
        spare = evens[3]
        spare, *_ = lax.optimization_barrier((spare, arrived))
        mates.append(xor_row(spare, 1))
        pairs = [block for one in zip(evens, mates) for block in one]
        last_tiles = [(tile, i) for i in (0, 2) for tile in pairs]
        links = [(tile, i) for i in (1, 3) for tile in pairs]
        side = jnp.stack([sent[:, wide:], arrived[:, wide:]])
        sent = (sent[:, :wide].astype(F32) + arrived[:, :wide].astype(F32)).astype(BF)
        link = functools.partial(link_kernel, R)
        sent, first = call(link, [sent, xor_col(sent, 2), side], links + last_tiles, [summed, (group, order)])
        turn = functools.partial(turn_kernel, R)
        sent, short = call(turn, [sent, xor_col(sent, 2)], last_tiles + links, [summed, (group, rows)])
        (sent,) = call(last_kernel, [first, short, sent, xor_col(sent, 2)], first_tiles, [(R * C,) + cut])
        remaining, back = pl.pallas_call(
            functools.partial(closing_kernel, C),
            out_shape=(
                jax.ShapeDtypeStruct(solved.shape, F32),
                jax.ShapeDtypeStruct((2, nrhs, rows), F32),
            ),
            compiler_params=PARAMS,
        )(solved, factor_rows, exchange(sent, ("row", "col")))
        return (back.transpose(0, 2, 1), remaining)

    return shards


def solution(mesh):
    R, C = mesh.shape["row"], mesh.shape["col"]

    def shards(factor_rows, solved, inverses, link_tile, right_side):
        group = solved.shape[0] // R
        aligned = group == 8 and inverses.shape[1] % 128 == 0 and inverses.shape[2] % 256 == 0
        build = tiled if aligned and C == 4 else generic
        return build(R, C)(factor_rows, solved, inverses, link_tile, right_side)

    placed = (
        P(None, None, ("row", "col")),
        P(None, ("row", "col")),
        P(None, "row", "col"),
        P("col", "row"),
        P(None, "col", None),
    )
    return jax.shard_map(
        shards,
        mesh=mesh,
        in_specs=placed,
        out_specs=(P(None, "col", None), P(None, ("row", "col"))),
        check_vma=False,
    )
```

```python
import functools

import jax
import jax.numpy as jnp
from jax import lax
from jax.experimental import pallas as pl
from jax.experimental.pallas import tpu as pltpu
from jax.sharding import Mesh
from jax.sharding import PartitionSpec as P

BF = jnp.bfloat16
F32 = jnp.float32
ROW = ("chip", "core")
PARAMS = pltpu.CompilerParams(vmem_limit_bytes=12 * 2**20)
WIDE = pltpu.CompilerParams(vmem_limit_bytes=62 * 2**20)


def dot(left, right, contract):
    return lax.dot_general(left, right, ((contract[0], contract[1]), ((), ())), preferred_element_type=F32)


def plain(left, right):
    return dot(left, right, ((1,), (0,)))


def flipped(left, right):
    return dot(left, right, ((1,), (1,)))


def exchange(value, axes):
    return lax.all_to_all(value, axes, 0, 0, tiled=False)


def generic(R, C):
    def xor_row(value, step):
        return lax.ppermute(value, "row", [(i, i ^ step) for i in range(R)])

    def sum_over_col(part):
        sent = jnp.broadcast_to(part.astype(BF)[None], (C,) + part.shape)
        return jnp.sum(exchange(sent, "col").astype(F32), axis=0)

    def shards(factor_rows, solved, inverses, link_tile, right_side):
        nrhs = solved.shape[0]
        group = nrhs // R
        rows = right_side.shape[1]
        order = rows * C
        own = jnp.concatenate([inverses, link_tile.T[None]], axis=0)
        near = [own] + [xor_row(own, step) for step in range(2, R, 2)]
        near = jnp.stack(near, axis=1)
        mate = xor_row(near, 1)
        weights = jnp.concatenate([near, mate], axis=1).reshape(3, order, rows)
        first_tile, last_tile, link_back = weights[0], weights[1], weights[2]

        part = jnp.einsum("nc,kic->nki", solved, factor_rows, preferred_element_type=F32).astype(BF)
        part = part.reshape(R, group, 2, C, rows).transpose(0, 3, 2, 1, 4).reshape(R * C, 2 * group, rows)
        panel = jnp.sum(exchange(part, ("row", "col")).astype(F32), axis=0).reshape(2, group, rows)
        mine = lax.dynamic_slice_in_dim(right_side, lax.axis_index("row") * group, group, 2)
        residue = mine.transpose(0, 2, 1) - panel

        first_solved = sum_over_col(flipped(residue[0].astype(BF), first_tile)).astype(BF)
        residue_last = (residue[1] - plain(first_solved, link_back)).astype(BF)
        last_solved = sum_over_col(flipped(residue_last, last_tile)).astype(BF)
        last_short = plain(last_solved, last_tile).astype(BF)
        back_term = sum_over_col(flipped(last_short, link_back))
        carry = (first_solved.astype(F32) - back_term).astype(BF)
        first_short = plain(carry, first_tile).astype(BF)

        both = jnp.concatenate([first_short, last_short], axis=0)
        sent = jnp.broadcast_to(both[None], (R * C,) + both.shape)
        whole = exchange(sent, ("row", "col")).reshape(R, C, 2, group, rows)
        whole = whole.transpose(2, 0, 3, 1, 4).reshape(2, nrhs, order)
        return finish(factor_rows, solved, (whole[0], whole[1]), rows)

    return shards


def finish(factor_rows, solved, both, rows):
    update = plain(both[0], factor_rows[0]) + plain(both[1], factor_rows[1])
    remaining = solved.astype(F32) - update
    here = [lax.dynamic_slice_in_dim(one, lax.axis_index("col") * rows, rows, 1) for one in both]
    return (jnp.stack([one.astype(F32).T for one in here]), remaining)


def fold(value):
    half = value.shape[-1] // 2
    return jnp.concatenate([value[..., :half], value[..., half:]], axis=-2)


def unfold(value):
    half = value.shape[-2] // 2
    return jnp.concatenate([value[..., :half, :], value[..., half:, :]], axis=-1)


def pack_kernel(inv_ref, link_ref, first_ref, pair_ref):
    first_ref[0] = inv_ref[0]
    pair_ref[0] = inv_ref[1]
    pair_ref[1] = link_ref[...].T


def stack_kernel(own_ref, far_ref, both_ref):
    both_ref[:2] = own_ref[...]
    both_ref[2:] = far_ref[...]


def panel_kernel(solved_ref, factor_ref, part_ref, solved, factor, sems):
    R, C, double, rows = part_ref.shape
    step = C // 4
    copies = [pltpu.make_async_copy(solved_ref, solved, sems.at[0])]
    for i in range(4):
        chunk = pl.ds(i * step * rows, step * rows)
        copies.append(pltpu.make_async_copy(factor_ref.at[:, chunk], factor.at[:, chunk], sems.at[1 + i]))
    for copy in copies:
        copy.start()
    copies[0].wait()
    value = solved[...]
    for c in range(C):
        if c % step == 0:
            copies[1 + c // step].wait()
        halves = [flipped(value, factor[k, c * rows : (c + 1) * rows]) for k in range(2)]
        halves = [half.reshape(R, double // 2, rows) for half in halves]
        part_ref[:, c] = jnp.concatenate(halves, axis=1).astype(BF)


def closing_kernel(C, solved_ref, factor_ref, own_ref, other_ref, remaining_ref, back_ref):
    chips = own_ref.shape[0] // C
    group, rows = own_ref.shape[1] // 2, own_ref.shape[2]
    even = lax.axis_index("core") == 0
    here = lax.axis_index("col")

    def columns(k, c):
        parts = []
        for chip in range(chips):
            own = own_ref[chip * C + c, k * group : (k + 1) * group].astype(F32)
            other = other_ref[chip * C + c, k * group : (k + 1) * group].astype(F32)
            parts += [jnp.where(even, own, other), jnp.where(even, other, own)]
        return jnp.concatenate(parts, axis=0)

    update = None
    for k in range(2):
        back_ref[k] = columns(k, here)
        for c in range(C):
            term = plain(columns(k, c).astype(BF), factor_ref[k, c * rows : (c + 1) * rows])
            update = term if update is None else update + term
    remaining_ref[...] = solved_ref[...].astype(F32) - update


def across(value, tiles):
    return jnp.concatenate([flipped(value, tile[0]) for tile in tiles], axis=1)


def along(value, tiles):
    size = tiles[0].shape[1]
    total = None
    for s, tile in enumerate(tiles):
        term = plain(value[:, s * size : (s + 1) * size], tile[0])
        total = term if total is None else total + term
    return total


def first_kernel(side_ref, panel_ref, *refs):
    tiles, sent_ref = refs[:-1], refs[-1]
    group = side_ref.shape[0] // 2
    total = panel_ref[0].astype(F32)
    for i in range(1, panel_ref.shape[0]):
        total += panel_ref[i].astype(F32)
    residue = side_ref[...] - total
    solved = across(residue[:group].astype(BF), tiles)
    sent_ref[...] = jnp.concatenate([fold(solved), fold(residue[group:])], axis=1).astype(BF)


def pair_sum(own_ref, other_ref):
    return unfold(own_ref[...].astype(F32) + other_ref[...].astype(F32))


def link_kernel(near, own_ref, other_ref, side_ref, *refs):
    links, last_tiles = refs[: 2 * near], refs[2 * near : 4 * near]
    sent_ref, first_ref = refs[4 * near :]
    first = pair_sum(own_ref, other_ref).astype(BF)
    first_ref[...] = first
    total = None
    for j in range(2):
        residue = unfold(side_ref[j].astype(F32)) - along(first, links[j * near : (j + 1) * near])
        term = across(residue.astype(BF), last_tiles[j * near : (j + 1) * near])
        total = term if total is None else total + term
    sent_ref[...] = fold(total).astype(BF)


def turn_kernel(near, own_ref, other_ref, *refs):
    last_tiles, links = refs[: 2 * near], refs[2 * near : 4 * near]
    sent_ref, short_ref = refs[4 * near :]
    last = pair_sum(own_ref, other_ref).astype(BF)
    total = None
    for j in range(2):
        short = along(last, last_tiles[j * near : (j + 1) * near]).astype(BF)
        if j == 0:
            short_ref[...] = short
        term = across(short, links[j * near : (j + 1) * near])
        total = term if total is None else total + term
    sent_ref[...] = fold(total).astype(BF)


def last_kernel(first_ref, short_ref, own_ref, other_ref, *refs):
    tiles, sent_ref = refs[:-1], refs[-1]
    carry = (first_ref[...].astype(F32) - pair_sum(own_ref, other_ref)).astype(BF)
    both = jnp.concatenate([along(carry, tiles), short_ref[...].astype(F32)], axis=0).astype(BF)
    for i in range(sent_ref.shape[0]):
        sent_ref[i] = both


def whole_spec(shape):
    return pl.BlockSpec(shape, lambda i: (0,) * len(shape))


def call(kernel, operands, tiles, shapes, params=PARAMS):
    def tile_spec(array, which):
        return pl.BlockSpec((1,) + array.shape[1:], lambda i: (which, 0, 0))

    return pl.pallas_call(
        kernel,
        grid=(1,),
        in_specs=[whole_spec(one.shape) for one in operands] + [tile_spec(*tile) for tile in tiles],
        out_specs=[whole_spec(shape) for shape in shapes],
        out_shape=[jax.ShapeDtypeStruct(shape, BF) for shape in shapes],
        compiler_params=params,
    )(*operands, *[tile[0] for tile in tiles])


def call_flat(kernel, operands, tiles, shapes):
    arrays = []
    for array, _ in tiles:
        if all(array is not one for one in arrays):
            arrays.append(array)
    places = [([array is one for one in arrays].index(True), which) for array, which in tiles]
    count = len(operands)

    def body(*refs):
        held = refs[count : count + len(arrays)]
        views = [held[i].at[pl.ds(which, 1)] for i, which in places]
        kernel(*refs[:count], *views, *refs[count + len(arrays) :])

    return pl.pallas_call(
        body,
        out_shape=[jax.ShapeDtypeStruct(shape, BF) for shape in shapes],
        compiler_params=PARAMS,
    )(*operands, *arrays)


def tiled(R, C):
    def xor_row(value, step):
        return lax.ppermute(value, ROW, [(i, i ^ step) for i in range(R)])

    def xor_col(value, step):
        return lax.ppermute(value, "col", [(i, i ^ step) for i in range(C)])

    def in_plane(value):
        return [value] + [xor_row(value, step) for step in range(2, R, 2)]

    def with_mates(evens):
        return [block for even in evens for block in (even, xor_row(even, 1))]

    def shards(factor_rows, solved, inverses, link_tile, right_side):
        nrhs = solved.shape[0]
        group = nrhs // R
        rows = right_side.shape[1]
        size = inverses.shape[1]
        order = rows * C
        cut = (2 * group, rows)

        first_own, pair = call(pack_kernel, [inverses, link_tile], [], [(1, size, rows), (2, size, rows)], WIDE)
        held = solved
        part = pl.pallas_call(
            panel_kernel,
            in_specs=[pl.BlockSpec(memory_space=pl.ANY)] * 2,
            out_shape=jax.ShapeDtypeStruct((R, C) + cut, BF),
            scratch_shapes=[
                pltpu.VMEM(solved.shape, BF),
                pltpu.VMEM(factor_rows.shape, BF),
                pltpu.SemaphoreType.DMA((5,)),
            ],
            compiler_params=WIDE,
        )(held, factor_rows)
        far = xor_col(pair, 1)
        first_in = first_own
        evens = in_plane(first_in)
        part, *_ = lax.optimization_barrier((part, far, *evens))
        panel = exchange(part.reshape((R * C,) + cut), ROW + ("col",))
        mine = lax.dynamic_slice_in_dim(right_side, lax.axis_index(ROW) * group, group, 2)
        mine = mine.transpose(0, 2, 1).reshape(cut)

        first_tiles = [(tile, 0) for tile in with_mates(evens)]
        own_pair = pair
        (both,) = call(stack_kernel, [own_pair, far], [], [(4, size, rows)])
        wide = order // 2
        summed = (2 * group, wide)
        (sent,) = call(first_kernel, [mine, panel], first_tiles, [(2 * group, wide + rows // 2)])
        evens = in_plane(both)
        arrived = xor_col(sent, 1)
        mates = []
        spare = evens[0]
        spare, *_ = lax.optimization_barrier((spare, arrived))
        mates.append(xor_row(spare, 1))
        spare = evens[1]
        spare, *_ = lax.optimization_barrier((spare, arrived))
        mates.append(xor_row(spare, 1))
        spare = evens[2]
        spare, *_ = lax.optimization_barrier((spare, arrived))
        mates.append(xor_row(spare, 1))
        spare = evens[3]
        spare, *_ = lax.optimization_barrier((spare, arrived))
        mates.append(xor_row(spare, 1))
        pairs = [block for one in zip(evens, mates) for block in one]
        last_tiles = [(tile, i) for i in (0, 2) for tile in pairs]
        links = [(tile, i) for i in (1, 3) for tile in pairs]
        side = jnp.stack([sent[:, wide:], arrived[:, wide:]])
        sent = (sent[:, :wide].astype(F32) + arrived[:, :wide].astype(F32)).astype(BF)
        link = functools.partial(link_kernel, R)
        sent, first = call_flat(link, [sent, xor_col(sent, 2), side], links + last_tiles, [summed, (group, order)])
        turn = functools.partial(turn_kernel, R)
        sent, short = call_flat(turn, [sent, xor_col(sent, 2)], last_tiles + links, [summed, (group, rows)])
        (sent,) = call_flat(last_kernel, [first, short, sent, xor_col(sent, 2)], first_tiles, [(R // 2 * C,) + cut])
        whole = exchange(sent, ("chip", "col"))
        remaining, back = pl.pallas_call(
            functools.partial(closing_kernel, C),
            out_shape=(
                jax.ShapeDtypeStruct(solved.shape, F32),
                jax.ShapeDtypeStruct((2, nrhs, rows), F32),
            ),
            compiler_params=PARAMS,
        )(solved, factor_rows, whole, xor_row(whole, 1))
        return (back.transpose(0, 2, 1), remaining)

    return shards


def solution(mesh):
    R, C = mesh.shape["row"], mesh.shape["col"]

    def whole(factor_rows, solved, inverses, link_tile, right_side):
        group, size, rows = solved.shape[0] // R, inverses.shape[1] // R, inverses.shape[2] // C
        if group == 8 and size % 128 == 0 and rows % 256 == 0 and C == 4 and R % 2 == 0:
            split, row, build = Mesh(mesh.devices.reshape(R // 2, 2, C), ROW + ("col",)), ROW, tiled
        else:
            split, row, build = mesh, ("row",), generic
        both = row + ("col",)
        placed = (P(None, None, both), P(None, both), P(None, row, "col"), P("col", row), P(None, "col", None))
        return jax.shard_map(
            build(R, C),
            mesh=split,
            in_specs=placed,
            out_specs=(P(None, "col", None), P(None, both)),
            check_vma=False,
        )(factor_rows, solved, inverses, link_tile, right_side)

    return whole
```

```python
import functools

import jax
import jax.numpy as jnp
from jax import lax
from jax.experimental import pallas as pl
from jax.experimental.pallas import tpu as pltpu
from jax.sharding import Mesh
from jax.sharding import PartitionSpec as P

BF = jnp.bfloat16
F32 = jnp.float32
ROW = ("chip", "core")
PARAMS = pltpu.CompilerParams(vmem_limit_bytes=12 * 2**20)
WIDE = pltpu.CompilerParams(vmem_limit_bytes=62 * 2**20)


def dot(left, right, contract):
    return lax.dot_general(left, right, ((contract[0], contract[1]), ((), ())), preferred_element_type=F32)


def plain(left, right):
    return dot(left, right, ((1,), (0,)))


def flipped(left, right):
    return dot(left, right, ((1,), (1,)))


def exchange(value, axes):
    return lax.all_to_all(value, axes, 0, 0, tiled=False)


def generic(R, C):
    def xor_row(value, step):
        return lax.ppermute(value, "row", [(i, i ^ step) for i in range(R)])

    def sum_over_col(part):
        sent = jnp.broadcast_to(part.astype(BF)[None], (C,) + part.shape)
        return jnp.sum(exchange(sent, "col").astype(F32), axis=0)

    def shards(factor_rows, solved, inverses, link_tile, right_side):
        nrhs = solved.shape[0]
        group = nrhs // R
        rows = right_side.shape[1]
        order = rows * C
        own = jnp.concatenate([inverses, link_tile.T[None]], axis=0)
        near = [own] + [xor_row(own, step) for step in range(2, R, 2)]
        near = jnp.stack(near, axis=1)
        mate = xor_row(near, 1)
        weights = jnp.concatenate([near, mate], axis=1).reshape(3, order, rows)
        first_tile, last_tile, link_back = weights[0], weights[1], weights[2]

        part = jnp.einsum("nc,kic->nki", solved, factor_rows, preferred_element_type=F32).astype(BF)
        part = part.reshape(R, group, 2, C, rows).transpose(0, 3, 2, 1, 4).reshape(R * C, 2 * group, rows)
        panel = jnp.sum(exchange(part, ("row", "col")).astype(F32), axis=0).reshape(2, group, rows)
        mine = lax.dynamic_slice_in_dim(right_side, lax.axis_index("row") * group, group, 2)
        residue = mine.transpose(0, 2, 1) - panel

        first_solved = sum_over_col(flipped(residue[0].astype(BF), first_tile)).astype(BF)
        residue_last = (residue[1] - plain(first_solved, link_back)).astype(BF)
        last_solved = sum_over_col(flipped(residue_last, last_tile)).astype(BF)
        last_short = plain(last_solved, last_tile).astype(BF)
        back_term = sum_over_col(flipped(last_short, link_back))
        carry = (first_solved.astype(F32) - back_term).astype(BF)
        first_short = plain(carry, first_tile).astype(BF)

        both = jnp.concatenate([first_short, last_short], axis=0)
        sent = jnp.broadcast_to(both[None], (R * C,) + both.shape)
        whole = exchange(sent, ("row", "col")).reshape(R, C, 2, group, rows)
        whole = whole.transpose(2, 0, 3, 1, 4).reshape(2, nrhs, order)
        return finish(factor_rows, solved, (whole[0], whole[1]), rows)

    return shards


def finish(factor_rows, solved, both, rows):
    update = plain(both[0], factor_rows[0]) + plain(both[1], factor_rows[1])
    remaining = solved.astype(F32) - update
    here = [lax.dynamic_slice_in_dim(one, lax.axis_index("col") * rows, rows, 1) for one in both]
    return (jnp.stack([one.astype(F32).T for one in here]), remaining)


def fold(value):
    half = value.shape[-1] // 2
    return jnp.concatenate([value[..., :half], value[..., half:]], axis=-2)


def unfold(value):
    half = value.shape[-2] // 2
    return jnp.concatenate([value[..., :half, :], value[..., half:, :]], axis=-1)


def pack_kernel(inv_ref, link_ref, pair_ref):
    pair_ref[0] = inv_ref[1]
    pair_ref[1] = link_ref[...].T


def stack_kernel(own_ref, far_ref, both_ref):
    both_ref[0] = own_ref[1]
    both_ref[1:] = far_ref[...]


def panel_kernel(solved_ref, factor_ref, part_ref, solved, factor, sems):
    R, C, double, rows = part_ref.shape
    step = C // 4
    copies = [pltpu.make_async_copy(solved_ref, solved, sems.at[0])]
    for i in range(4):
        chunk = pl.ds(i * step * rows, step * rows)
        copies.append(pltpu.make_async_copy(factor_ref.at[:, chunk], factor.at[:, chunk], sems.at[1 + i]))
    for copy in copies:
        copy.start()
    copies[0].wait()
    value = solved[...]
    for c in range(C):
        if c % step == 0:
            copies[1 + c // step].wait()
        halves = [flipped(value, factor[k, c * rows : (c + 1) * rows]) for k in range(2)]
        halves = [half.reshape(R, double // 2, rows) for half in halves]
        part_ref[:, c] = jnp.concatenate(halves, axis=1).astype(BF)


def closing_kernel(C, solved_ref, factor_ref, own_ref, other_ref, remaining_ref, back_ref):
    chips = own_ref.shape[0] // C
    group, rows = own_ref.shape[1] // 2, own_ref.shape[2]
    even = lax.axis_index("core") == 0
    here = lax.axis_index("col")

    def columns(k, c):
        parts = []
        for chip in range(chips):
            own = own_ref[chip * C + c, k * group : (k + 1) * group].astype(F32)
            other = other_ref[chip * C + c, k * group : (k + 1) * group].astype(F32)
            parts += [jnp.where(even, own, other), jnp.where(even, other, own)]
        return jnp.concatenate(parts, axis=0)

    update = None
    for k in range(2):
        back_ref[k] = columns(k, here)
        for c in range(C):
            term = plain(columns(k, c).astype(BF), factor_ref[k, c * rows : (c + 1) * rows])
            update = term if update is None else update + term
    remaining_ref[...] = solved_ref[...].astype(F32) - update


def across(value, tiles):
    return jnp.concatenate([flipped(value, tile[0]) for tile in tiles], axis=1)


def along(value, tiles):
    size = tiles[0].shape[1]
    total = None
    for s, tile in enumerate(tiles):
        term = plain(value[:, s * size : (s + 1) * size], tile[0])
        total = term if total is None else total + term
    return total


def first_kernel(side_ref, panel_ref, *refs):
    tiles, sent_ref = refs[:-1], refs[-1]
    group = side_ref.shape[0] // 2
    total = panel_ref[0].astype(F32)
    for i in range(1, panel_ref.shape[0]):
        total += panel_ref[i].astype(F32)
    residue = side_ref[...] - total
    solved = across(residue[:group].astype(BF), tiles)
    sent_ref[...] = jnp.concatenate([fold(solved), fold(residue[group:])], axis=1).astype(BF)


def pair_sum(own_ref, other_ref):
    return unfold(own_ref[...].astype(F32) + other_ref[...].astype(F32))


def link_kernel(near, own_ref, other_ref, side_ref, *refs):
    links, last_tiles = refs[: 2 * near], refs[2 * near : 4 * near]
    sent_ref, first_ref = refs[4 * near :]
    first = pair_sum(own_ref, other_ref).astype(BF)
    first_ref[...] = first
    total = None
    for j in range(2):
        residue = unfold(side_ref[j].astype(F32)) - along(first, links[j * near : (j + 1) * near])
        term = across(residue.astype(BF), last_tiles[j * near : (j + 1) * near])
        total = term if total is None else total + term
    sent_ref[...] = fold(total).astype(BF)


def turn_kernel(near, own_ref, other_ref, *refs):
    last_tiles, links = refs[: 2 * near], refs[2 * near : 4 * near]
    sent_ref, short_ref = refs[4 * near :]
    last = pair_sum(own_ref, other_ref).astype(BF)
    total = None
    for j in range(2):
        short = along(last, last_tiles[j * near : (j + 1) * near]).astype(BF)
        if j == 0:
            short_ref[...] = short
        term = across(short, links[j * near : (j + 1) * near])
        total = term if total is None else total + term
    sent_ref[...] = fold(total).astype(BF)


def last_kernel(first_ref, short_ref, own_ref, other_ref, *refs):
    tiles, sent_ref = refs[:-1], refs[-1]
    carry = (first_ref[...].astype(F32) - pair_sum(own_ref, other_ref)).astype(BF)
    both = jnp.concatenate([along(carry, tiles), short_ref[...].astype(F32)], axis=0).astype(BF)
    for i in range(sent_ref.shape[0]):
        sent_ref[i] = both


def whole_spec(shape):
    return pl.BlockSpec(shape, lambda i: (0,) * len(shape))


def call(kernel, operands, tiles, shapes, params=PARAMS):
    def tile_spec(array, which):
        return pl.BlockSpec((1,) + array.shape[1:], lambda i: (which, 0, 0))

    return pl.pallas_call(
        kernel,
        grid=(1,),
        in_specs=[whole_spec(one.shape) for one in operands] + [tile_spec(*tile) for tile in tiles],
        out_specs=[whole_spec(shape) for shape in shapes],
        out_shape=[jax.ShapeDtypeStruct(shape, BF) for shape in shapes],
        compiler_params=params,
    )(*operands, *[tile[0] for tile in tiles])


def call_flat(kernel, operands, tiles, shapes):
    arrays = []
    for array, _ in tiles:
        if all(array is not one for one in arrays):
            arrays.append(array)
    places = [([array is one for one in arrays].index(True), which) for array, which in tiles]
    count = len(operands)

    def body(*refs):
        held = refs[count : count + len(arrays)]
        views = [held[i].at[pl.ds(which, 1)] for i, which in places]
        kernel(*refs[:count], *views, *refs[count + len(arrays) :])

    return pl.pallas_call(
        body,
        out_shape=[jax.ShapeDtypeStruct(shape, BF) for shape in shapes],
        compiler_params=PARAMS,
    )(*operands, *arrays)


def tiled(R, C):
    def xor_row(value, step):
        return lax.ppermute(value, ROW, [(i, i ^ step) for i in range(R)])

    def xor_col(value, step):
        return lax.ppermute(value, "col", [(i, i ^ step) for i in range(C)])

    def in_plane(value):
        return [value] + [xor_row(value, step) for step in range(2, R, 2)]

    def with_mates(evens):
        return [block for even in evens for block in (even, xor_row(even, 1))]

    def shards(factor_rows, solved, inverses, link_tile, right_side):
        nrhs = solved.shape[0]
        group = nrhs // R
        rows = right_side.shape[1]
        size = inverses.shape[1]
        order = rows * C
        cut = (2 * group, rows)

        (pair,) = call(pack_kernel, [inverses, link_tile], [], [(2, size, rows)], WIDE)
        held = solved
        held, *_ = lax.optimization_barrier((held, pair))
        part = pl.pallas_call(
            panel_kernel,
            in_specs=[pl.BlockSpec(memory_space=pl.ANY)] * 2,
            out_shape=jax.ShapeDtypeStruct((R, C) + cut, BF),
            scratch_shapes=[
                pltpu.VMEM(solved.shape, BF),
                pltpu.VMEM(factor_rows.shape, BF),
                pltpu.SemaphoreType.DMA((5,)),
            ],
            compiler_params=WIDE,
        )(held, factor_rows)
        far = xor_col(pair, 2)
        first_in = inverses
        evens = in_plane(first_in)
        part, *_ = lax.optimization_barrier((part, far, *evens))
        panel = exchange(part.reshape((R * C,) + cut), ROW + ("col",))
        mine = lax.dynamic_slice_in_dim(right_side, lax.axis_index(ROW) * group, group, 2)
        mine = mine.transpose(0, 2, 1).reshape(cut)

        own = with_mates(evens)
        first_tiles = [(tile, 0) for tile in own]
        own_pair = pair
        (both,) = call(stack_kernel, [own_pair, far], [], [(3, size, rows)])
        wide = order // 2
        summed = (2 * group, wide)
        (sent,) = call(first_kernel, [mine, panel], first_tiles, [(2 * group, wide + rows // 2)])
        evens = in_plane(both)
        arrived = xor_col(sent, 2)
        mates = []
        spare = evens[0]
        spare, *_ = lax.optimization_barrier((spare, arrived))
        mates.append(xor_row(spare, 1))
        spare = evens[1]
        spare, *_ = lax.optimization_barrier((spare, arrived))
        mates.append(xor_row(spare, 1))
        spare = evens[2]
        spare, *_ = lax.optimization_barrier((spare, arrived))
        mates.append(xor_row(spare, 1))
        spare = evens[3]
        spare, *_ = lax.optimization_barrier((spare, arrived))
        mates.append(xor_row(spare, 1))
        pairs = [block for one in zip(evens, mates) for block in one]
        last_tiles = [(tile, 1) for tile in own] + [(tile, 1) for tile in pairs]
        links = [(tile, i) for i in (0, 2) for tile in pairs]
        side = jnp.stack([sent[:, wide:], arrived[:, wide:]])
        sent = (sent[:, :wide].astype(F32) + arrived[:, :wide].astype(F32)).astype(BF)
        link = functools.partial(link_kernel, R)
        sent, first = call_flat(link, [sent, xor_col(sent, 1), side], links + last_tiles, [summed, (group, order)])
        turn = functools.partial(turn_kernel, R)
        sent, short = call_flat(turn, [sent, xor_col(sent, 1)], last_tiles + links, [summed, (group, rows)])
        (sent,) = call_flat(last_kernel, [first, short, sent, xor_col(sent, 1)], first_tiles, [(R // 2 * C,) + cut])
        whole = exchange(sent, ("chip", "col"))
        remaining, back = pl.pallas_call(
            functools.partial(closing_kernel, C),
            out_shape=(
                jax.ShapeDtypeStruct(solved.shape, F32),
                jax.ShapeDtypeStruct((2, nrhs, rows), F32),
            ),
            compiler_params=PARAMS,
        )(solved, factor_rows, whole, xor_row(whole, 1))
        return (back.transpose(0, 2, 1), remaining)

    return shards


def solution(mesh):
    R, C = mesh.shape["row"], mesh.shape["col"]

    def whole(factor_rows, solved, inverses, link_tile, right_side):
        group, size, rows = solved.shape[0] // R, inverses.shape[1] // R, inverses.shape[2] // C
        if group == 8 and size % 128 == 0 and rows % 256 == 0 and C == 4 and R % 2 == 0:
            split, row, build = Mesh(mesh.devices.reshape(R // 2, 2, C), ROW + ("col",)), ROW, tiled
        else:
            split, row, build = mesh, ("row",), generic
        both = row + ("col",)
        placed = (P(None, None, both), P(None, both), P(None, row, "col"), P("col", row), P(None, "col", None))
        return jax.shard_map(
            build(R, C),
            mesh=split,
            in_specs=placed,
            out_specs=(P(None, "col", None), P(None, both)),
            check_vma=False,
        )(factor_rows, solved, inverses, link_tile, right_side)

    return whole
```

```python
import functools

import jax
import jax.numpy as jnp
from jax import lax
from jax.experimental import pallas as pl
from jax.experimental.pallas import tpu as pltpu
from jax.sharding import Mesh
from jax.sharding import PartitionSpec as P

BF = jnp.bfloat16
F32 = jnp.float32
ROW = ("chip", "core")
PARAMS = pltpu.CompilerParams(vmem_limit_bytes=12 * 2**20)
WIDE = pltpu.CompilerParams(vmem_limit_bytes=62 * 2**20)


def dot(left, right, contract):
    return lax.dot_general(left, right, ((contract[0], contract[1]), ((), ())), preferred_element_type=F32)


def plain(left, right):
    return dot(left, right, ((1,), (0,)))


def flipped(left, right):
    return dot(left, right, ((1,), (1,)))


def exchange(value, axes):
    return lax.all_to_all(value, axes, 0, 0, tiled=False)


def generic(R, C):
    def xor_row(value, step):
        return lax.ppermute(value, "row", [(i, i ^ step) for i in range(R)])

    def sum_over_col(part):
        sent = jnp.broadcast_to(part.astype(BF)[None], (C,) + part.shape)
        return jnp.sum(exchange(sent, "col").astype(F32), axis=0)

    def shards(factor_rows, solved, inverses, link_tile, right_side):
        nrhs = solved.shape[0]
        group = nrhs // R
        rows = right_side.shape[1]
        order = rows * C
        own = jnp.concatenate([inverses, link_tile.T[None]], axis=0)
        near = [own] + [xor_row(own, step) for step in range(2, R, 2)]
        near = jnp.stack(near, axis=1)
        mate = xor_row(near, 1)
        weights = jnp.concatenate([near, mate], axis=1).reshape(3, order, rows)
        first_tile, last_tile, link_back = weights[0], weights[1], weights[2]

        part = jnp.einsum("nc,kic->nki", solved, factor_rows, preferred_element_type=F32).astype(BF)
        part = part.reshape(R, group, 2, C, rows).transpose(0, 3, 2, 1, 4).reshape(R * C, 2 * group, rows)
        panel = jnp.sum(exchange(part, ("row", "col")).astype(F32), axis=0).reshape(2, group, rows)
        mine = lax.dynamic_slice_in_dim(right_side, lax.axis_index("row") * group, group, 2)
        residue = mine.transpose(0, 2, 1) - panel

        first_solved = sum_over_col(flipped(residue[0].astype(BF), first_tile)).astype(BF)
        residue_last = (residue[1] - plain(first_solved, link_back)).astype(BF)
        last_solved = sum_over_col(flipped(residue_last, last_tile)).astype(BF)
        last_short = plain(last_solved, last_tile).astype(BF)
        back_term = sum_over_col(flipped(last_short, link_back))
        carry = (first_solved.astype(F32) - back_term).astype(BF)
        first_short = plain(carry, first_tile).astype(BF)

        both = jnp.concatenate([first_short, last_short], axis=0)
        sent = jnp.broadcast_to(both[None], (R * C,) + both.shape)
        whole = exchange(sent, ("row", "col")).reshape(R, C, 2, group, rows)
        whole = whole.transpose(2, 0, 3, 1, 4).reshape(2, nrhs, order)
        return finish(factor_rows, solved, (whole[0], whole[1]), rows)

    return shards


def finish(factor_rows, solved, both, rows):
    update = plain(both[0], factor_rows[0]) + plain(both[1], factor_rows[1])
    remaining = solved.astype(F32) - update
    here = [lax.dynamic_slice_in_dim(one, lax.axis_index("col") * rows, rows, 1) for one in both]
    return (jnp.stack([one.astype(F32).T for one in here]), remaining)


def fold(value):
    half = value.shape[-1] // 2
    return jnp.concatenate([value[..., :half], value[..., half:]], axis=-2)


def unfold(value):
    half = value.shape[-2] // 2
    return jnp.concatenate([value[..., :half, :], value[..., half:, :]], axis=-1)


def pack_kernel(inv_ref, link_ref, pair_ref):
    pair_ref[0] = inv_ref[1]
    pair_ref[1] = link_ref[...].T


def stack_kernel(own_ref, far_ref, both_ref):
    both_ref[0] = own_ref[1]
    both_ref[1:] = far_ref[...]


def panel_kernel(solved_ref, factor_ref, part_ref, solved, factor, sems):
    R, C, double, rows = part_ref.shape
    step = C // 4
    copies = [pltpu.make_async_copy(solved_ref, solved, sems.at[0])]
    for i in range(4):
        chunk = pl.ds(i * step * rows, step * rows)
        copies.append(pltpu.make_async_copy(factor_ref.at[:, chunk], factor.at[:, chunk], sems.at[1 + i]))
    for copy in copies:
        copy.start()
    copies[0].wait()
    value = solved[...]
    for c in range(C):
        if c % step == 0:
            copies[1 + c // step].wait()
        halves = [flipped(value, factor[k, c * rows : (c + 1) * rows]) for k in range(2)]
        halves = [half.reshape(R, double // 2, rows) for half in halves]
        part_ref[:, c] = jnp.concatenate(halves, axis=1).astype(BF)


def closing_kernel(C, solved_ref, factor_ref, own_ref, other_ref, remaining_ref, back_ref):
    chips = own_ref.shape[0] // C
    group, rows = own_ref.shape[1] // 2, own_ref.shape[2]
    even = lax.axis_index("core") == 0
    here = lax.axis_index("col")

    def columns(k, c):
        parts = []
        for chip in range(chips):
            own = own_ref[chip * C + c, k * group : (k + 1) * group].astype(F32)
            other = other_ref[chip * C + c, k * group : (k + 1) * group].astype(F32)
            parts += [jnp.where(even, own, other), jnp.where(even, other, own)]
        return jnp.concatenate(parts, axis=0)

    update = None
    for k in range(2):
        back_ref[k] = columns(k, here)
        for c in range(C):
            term = plain(columns(k, c).astype(BF), factor_ref[k, c * rows : (c + 1) * rows])
            update = term if update is None else update + term
    remaining_ref[...] = solved_ref[...].astype(F32) - update


def stacked(tiles):
    return jnp.concatenate([tile[0] for tile in tiles], axis=0)


def across(value, tiles):
    return flipped(value, stacked(tiles))


def along(value, tiles):
    return plain(value, stacked(tiles))


def first_kernel(side_ref, panel_ref, *refs):
    tiles, sent_ref = refs[:-1], refs[-1]
    group = side_ref.shape[0] // 2
    total = panel_ref[0].astype(F32)
    for i in range(1, panel_ref.shape[0]):
        total += panel_ref[i].astype(F32)
    residue = side_ref[...] - total
    solved = across(residue[:group].astype(BF), tiles)
    sent_ref[...] = jnp.concatenate([fold(solved), fold(residue[group:])], axis=1).astype(BF)


def pair_sum(own_ref, other_ref):
    return unfold(own_ref[...].astype(F32) + other_ref[...].astype(F32))


def link_kernel(near, own_ref, other_ref, side_ref, *refs):
    links, last_tiles = refs[: 2 * near], refs[2 * near : 4 * near]
    sent_ref, first_ref = refs[4 * near :]
    first = pair_sum(own_ref, other_ref).astype(BF)
    first_ref[...] = first
    total = None
    for j in range(2):
        residue = unfold(side_ref[j].astype(F32)) - along(first, links[j * near : (j + 1) * near])
        term = across(residue.astype(BF), last_tiles[j * near : (j + 1) * near])
        total = term if total is None else total + term
    sent_ref[...] = fold(total).astype(BF)


def turn_kernel(near, own_ref, other_ref, *refs):
    last_tiles, links = refs[: 2 * near], refs[2 * near : 4 * near]
    sent_ref, short_ref = refs[4 * near :]
    last = pair_sum(own_ref, other_ref).astype(BF)
    total = None
    for j in range(2):
        short = along(last, last_tiles[j * near : (j + 1) * near]).astype(BF)
        if j == 0:
            short_ref[...] = short
        term = across(short, links[j * near : (j + 1) * near])
        total = term if total is None else total + term
    sent_ref[...] = fold(total).astype(BF)


def last_kernel(first_ref, short_ref, own_ref, other_ref, *refs):
    tiles, sent_ref = refs[:-1], refs[-1]
    carry = (first_ref[...].astype(F32) - pair_sum(own_ref, other_ref)).astype(BF)
    both = jnp.concatenate([along(carry, tiles), short_ref[...].astype(F32)], axis=0).astype(BF)
    for i in range(sent_ref.shape[0]):
        sent_ref[i] = both


def whole_spec(shape):
    return pl.BlockSpec(shape, lambda i: (0,) * len(shape))


def call(kernel, operands, tiles, shapes, params=PARAMS):
    def tile_spec(array, which):
        return pl.BlockSpec((1,) + array.shape[1:], lambda i: (which, 0, 0))

    return pl.pallas_call(
        kernel,
        grid=(1,),
        in_specs=[whole_spec(one.shape) for one in operands] + [tile_spec(*tile) for tile in tiles],
        out_specs=[whole_spec(shape) for shape in shapes],
        out_shape=[jax.ShapeDtypeStruct(shape, BF) for shape in shapes],
        compiler_params=params,
    )(*operands, *[tile[0] for tile in tiles])


def call_flat(kernel, operands, tiles, shapes):
    arrays = []
    for array, _ in tiles:
        if all(array is not one for one in arrays):
            arrays.append(array)
    places = [([array is one for one in arrays].index(True), which) for array, which in tiles]
    count = len(operands)

    def body(*refs):
        held = refs[count : count + len(arrays)]
        views = [held[i].at[pl.ds(which, 1)] for i, which in places]
        kernel(*refs[:count], *views, *refs[count + len(arrays) :])

    return pl.pallas_call(
        body,
        out_shape=[jax.ShapeDtypeStruct(shape, BF) for shape in shapes],
        compiler_params=PARAMS,
    )(*operands, *arrays)


def tiled(R, C):
    def xor_row(value, step):
        return lax.ppermute(value, ROW, [(i, i ^ step) for i in range(R)])

    def xor_col(value, step):
        return lax.ppermute(value, "col", [(i, i ^ step) for i in range(C)])

    def in_plane(value):
        return [value] + [xor_row(value, step) for step in range(2, R, 2)]

    def with_mates(evens):
        return [block for even in evens for block in (even, xor_row(even, 1))]

    def shards(factor_rows, solved, inverses, link_tile, right_side):
        nrhs = solved.shape[0]
        group = nrhs // R
        rows = right_side.shape[1]
        size = inverses.shape[1]
        order = rows * C
        cut = (2 * group, rows)

        (pair,) = call(pack_kernel, [inverses, link_tile], [], [(2, size, rows)], WIDE)
        held = solved
        held, *_ = lax.optimization_barrier((held, pair))
        part = pl.pallas_call(
            panel_kernel,
            in_specs=[pl.BlockSpec(memory_space=pl.ANY)] * 2,
            out_shape=jax.ShapeDtypeStruct((R, C) + cut, BF),
            scratch_shapes=[
                pltpu.VMEM(solved.shape, BF),
                pltpu.VMEM(factor_rows.shape, BF),
                pltpu.SemaphoreType.DMA((5,)),
            ],
            compiler_params=WIDE,
        )(held, factor_rows)
        far = xor_col(pair, 2)
        first_in = inverses
        evens = in_plane(first_in)
        part, *_ = lax.optimization_barrier((part, far, *evens))
        panel = exchange(part.reshape((R * C,) + cut), ROW + ("col",))
        mine = lax.dynamic_slice_in_dim(right_side, lax.axis_index(ROW) * group, group, 2)
        mine = mine.transpose(0, 2, 1).reshape(cut)

        own = with_mates(evens)
        first_tiles = [(tile, 0) for tile in own]
        own_pair = pair
        (both,) = call(stack_kernel, [own_pair, far], [], [(3, size, rows)])
        wide = order // 2
        summed = (2 * group, wide)
        (sent,) = call(first_kernel, [mine, panel], first_tiles, [(2 * group, wide + rows // 2)])
        evens = in_plane(both)
        arrived = xor_col(sent, 2)
        mates = []
        spare = evens[0]
        spare, *_ = lax.optimization_barrier((spare, arrived))
        mates.append(xor_row(spare, 1))
        spare = evens[1]
        spare, *_ = lax.optimization_barrier((spare, arrived))
        mates.append(xor_row(spare, 1))
        spare = evens[2]
        spare, *_ = lax.optimization_barrier((spare, arrived))
        mates.append(xor_row(spare, 1))
        spare = evens[3]
        spare, *_ = lax.optimization_barrier((spare, arrived))
        mates.append(xor_row(spare, 1))
        pairs = [block for one in zip(evens, mates) for block in one]
        last_tiles = [(tile, 1) for tile in own] + [(tile, 1) for tile in pairs]
        links = [(tile, i) for i in (0, 2) for tile in pairs]
        side = jnp.stack([sent[:, wide:], arrived[:, wide:]])
        sent = (sent[:, :wide].astype(F32) + arrived[:, :wide].astype(F32)).astype(BF)
        link = functools.partial(link_kernel, R)
        sent, first = call_flat(link, [sent, xor_col(sent, 1), side], links + last_tiles, [summed, (group, order)])
        turn = functools.partial(turn_kernel, R)
        sent, short = call_flat(turn, [sent, xor_col(sent, 1)], last_tiles + links, [summed, (group, rows)])
        (sent,) = call_flat(last_kernel, [first, short, sent, xor_col(sent, 1)], first_tiles, [(R // 2 * C,) + cut])
        whole = exchange(sent, ("chip", "col"))
        remaining, back = pl.pallas_call(
            functools.partial(closing_kernel, C),
            out_shape=(
                jax.ShapeDtypeStruct(solved.shape, F32),
                jax.ShapeDtypeStruct((2, nrhs, rows), F32),
            ),
            compiler_params=PARAMS,
        )(solved, factor_rows, whole, xor_row(whole, 1))
        return (back.transpose(0, 2, 1), remaining)

    return shards


def solution(mesh):
    R, C = mesh.shape["row"], mesh.shape["col"]

    def whole(factor_rows, solved, inverses, link_tile, right_side):
        group, size, rows = solved.shape[0] // R, inverses.shape[1] // R, inverses.shape[2] // C
        if group == 8 and size % 128 == 0 and rows % 256 == 0 and C == 4 and R % 2 == 0:
            split, row, build = Mesh(mesh.devices.reshape(R // 2, 2, C), ROW + ("col",)), ROW, tiled
        else:
            split, row, build = mesh, ("row",), generic
        both = row + ("col",)
        placed = (P(None, None, both), P(None, both), P(None, row, "col"), P("col", row), P(None, "col", None))
        return jax.shard_map(
            build(R, C),
            mesh=split,
            in_specs=placed,
            out_specs=(P(None, "col", None), P(None, both)),
            check_vma=False,
        )(factor_rows, solved, inverses, link_tile, right_side)

    return whole
```

```python
import functools

import jax
import jax.numpy as jnp
from jax import lax
from jax.experimental import pallas as pl
from jax.experimental.pallas import tpu as pltpu
from jax.sharding import Mesh
from jax.sharding import PartitionSpec as P

BF = jnp.bfloat16
F32 = jnp.float32
ROW = ("chip", "core")
PARAMS = pltpu.CompilerParams(vmem_limit_bytes=12 * 2**20)
WIDE = pltpu.CompilerParams(vmem_limit_bytes=62 * 2**20)


def dot(left, right, contract):
    return lax.dot_general(left, right, ((contract[0], contract[1]), ((), ())), preferred_element_type=F32)


def plain(left, right):
    return dot(left, right, ((1,), (0,)))


def flipped(left, right):
    return dot(left, right, ((1,), (1,)))


def exchange(value, axes):
    return lax.all_to_all(value, axes, 0, 0, tiled=False)


def generic(R, C):
    def xor_row(value, step):
        return lax.ppermute(value, "row", [(i, i ^ step) for i in range(R)])

    def sum_over_col(part):
        sent = jnp.broadcast_to(part.astype(BF)[None], (C,) + part.shape)
        return jnp.sum(exchange(sent, "col").astype(F32), axis=0)

    def shards(factor_rows, solved, inverses, link_tile, right_side):
        nrhs = solved.shape[0]
        group = nrhs // R
        rows = right_side.shape[1]
        order = rows * C
        own = jnp.concatenate([inverses, link_tile.T[None]], axis=0)
        near = [own] + [xor_row(own, step) for step in range(2, R, 2)]
        near = jnp.stack(near, axis=1)
        mate = xor_row(near, 1)
        weights = jnp.concatenate([near, mate], axis=1).reshape(3, order, rows)
        first_tile, last_tile, link_back = weights[0], weights[1], weights[2]

        part = jnp.einsum("nc,kic->nki", solved, factor_rows, preferred_element_type=F32).astype(BF)
        part = part.reshape(R, group, 2, C, rows).transpose(0, 3, 2, 1, 4).reshape(R * C, 2 * group, rows)
        panel = jnp.sum(exchange(part, ("row", "col")).astype(F32), axis=0).reshape(2, group, rows)
        mine = lax.dynamic_slice_in_dim(right_side, lax.axis_index("row") * group, group, 2)
        residue = mine.transpose(0, 2, 1) - panel

        first_solved = sum_over_col(flipped(residue[0].astype(BF), first_tile)).astype(BF)
        residue_last = (residue[1] - plain(first_solved, link_back)).astype(BF)
        last_solved = sum_over_col(flipped(residue_last, last_tile)).astype(BF)
        last_short = plain(last_solved, last_tile).astype(BF)
        back_term = sum_over_col(flipped(last_short, link_back))
        carry = (first_solved.astype(F32) - back_term).astype(BF)
        first_short = plain(carry, first_tile).astype(BF)

        both = jnp.concatenate([first_short, last_short], axis=0)
        sent = jnp.broadcast_to(both[None], (R * C,) + both.shape)
        whole = exchange(sent, ("row", "col")).reshape(R, C, 2, group, rows)
        whole = whole.transpose(2, 0, 3, 1, 4).reshape(2, nrhs, order)
        return finish(factor_rows, solved, (whole[0], whole[1]), rows)

    return shards


def finish(factor_rows, solved, both, rows):
    update = plain(both[0], factor_rows[0]) + plain(both[1], factor_rows[1])
    remaining = solved.astype(F32) - update
    here = [lax.dynamic_slice_in_dim(one, lax.axis_index("col") * rows, rows, 1) for one in both]
    return (jnp.stack([one.astype(F32).T for one in here]), remaining)


def fold(value):
    half = value.shape[-1] // 2
    return jnp.concatenate([value[..., :half], value[..., half:]], axis=-2)


def unfold(value):
    half = value.shape[-2] // 2
    return jnp.concatenate([value[..., :half, :], value[..., half:, :]], axis=-1)


def pack_kernel(inv_ref, link_ref, pair_ref):
    pair_ref[0] = inv_ref[1]
    pair_ref[1] = link_ref[...].T


def stack_kernel(own_ref, far_ref, both_ref):
    both_ref[0] = own_ref[1]
    both_ref[1:] = far_ref[...]


def panel_kernel(solved_ref, factor_ref, part_ref, solved, factor, sems):
    R, C, double, rows = part_ref.shape
    step = C // 4
    copies = [pltpu.make_async_copy(solved_ref, solved, sems.at[0])]
    for i in range(4):
        chunk = pl.ds(i * step * rows, step * rows)
        copies.append(pltpu.make_async_copy(factor_ref.at[:, chunk], factor.at[:, chunk], sems.at[1 + i]))
    for copy in copies:
        copy.start()
    copies[0].wait()
    value = solved[...]
    for c in range(C):
        if c % step == 0:
            copies[1 + c // step].wait()
        halves = [flipped(value, factor[k, c * rows : (c + 1) * rows]) for k in range(2)]
        halves = [half.reshape(R, double // 2, rows) for half in halves]
        part_ref[:, c] = jnp.concatenate(halves, axis=1).astype(BF)


def closing_kernel(C, solved_ref, factor_ref, own_ref, other_ref, remaining_ref, back_ref):
    chips = own_ref.shape[0] // C
    group, rows = own_ref.shape[1] // 2, own_ref.shape[2]
    even = lax.axis_index("core") == 0
    here = lax.axis_index("col")

    def columns(k, c):
        parts = []
        for chip in range(chips):
            own = own_ref[chip * C + c, k * group : (k + 1) * group].astype(F32)
            other = other_ref[chip * C + c, k * group : (k + 1) * group].astype(F32)
            parts += [jnp.where(even, own, other), jnp.where(even, other, own)]
        return jnp.concatenate(parts, axis=0)

    update = None
    for k in range(2):
        back_ref[k] = columns(k, here)
        for c in range(C):
            term = plain(columns(k, c).astype(BF), factor_ref[k, c * rows : (c + 1) * rows])
            update = term if update is None else update + term
    remaining_ref[...] = solved_ref[...].astype(F32) - update


def stacked(tiles):
    return jnp.concatenate([tile[0] for tile in tiles], axis=0)


def across(value, tiles):
    return flipped(value, stacked(tiles))


def along(value, tiles):
    return plain(value, stacked(tiles))


def first_kernel(side_ref, panel_ref, *refs):
    tiles, sent_ref = refs[:-1], refs[-1]
    group = side_ref.shape[0] // 2
    total = panel_ref[0].astype(F32)
    for i in range(1, panel_ref.shape[0]):
        total += panel_ref[i].astype(F32)
    residue = side_ref[...] - total
    solved = across(residue[:group].astype(BF), tiles)
    sent_ref[...] = jnp.concatenate([fold(solved), fold(residue[group:])], axis=1).astype(BF)


def pair_sum(own_ref, other_ref):
    return unfold(own_ref[...].astype(F32) + other_ref[...].astype(F32))


def link_kernel(near, own_ref, other_ref, side_ref, *refs):
    links, last_tiles = refs[: 2 * near], refs[2 * near : 4 * near]
    sent_ref, first_ref = refs[4 * near :]
    first = pair_sum(own_ref, other_ref).astype(BF)
    first_ref[...] = first
    total = None
    for j in range(2):
        residue = unfold(side_ref[j].astype(F32)) - along(first, links[j * near : (j + 1) * near])
        term = across(residue.astype(BF), last_tiles[j * near : (j + 1) * near])
        total = term if total is None else total + term
    sent_ref[...] = fold(total).astype(BF)


def turn_kernel(near, own_ref, other_ref, *refs):
    last_tiles, links = refs[: 2 * near], refs[2 * near : 4 * near]
    sent_ref, short_ref = refs[4 * near :]
    last = pair_sum(own_ref, other_ref).astype(BF)
    total = None
    for j in range(2):
        short = along(last, last_tiles[j * near : (j + 1) * near]).astype(BF)
        if j == 0:
            short_ref[...] = short
        term = across(short, links[j * near : (j + 1) * near])
        total = term if total is None else total + term
    sent_ref[...] = fold(total).astype(BF)


def last_kernel(first_ref, short_ref, own_ref, other_ref, *refs):
    tiles, sent_ref = refs[:-1], refs[-1]
    carry = (first_ref[...].astype(F32) - pair_sum(own_ref, other_ref)).astype(BF)
    both = jnp.concatenate([along(carry, tiles), short_ref[...].astype(F32)], axis=0).astype(BF)
    for i in range(sent_ref.shape[0]):
        sent_ref[i] = both


def whole_spec(shape):
    return pl.BlockSpec(shape, lambda i: (0,) * len(shape))


def call(kernel, operands, tiles, shapes, params=PARAMS):
    def tile_spec(array, which):
        return pl.BlockSpec((1,) + array.shape[1:], lambda i: (which, 0, 0))

    return pl.pallas_call(
        kernel,
        grid=(1,),
        in_specs=[whole_spec(one.shape) for one in operands] + [tile_spec(*tile) for tile in tiles],
        out_specs=[whole_spec(shape) for shape in shapes],
        out_shape=[jax.ShapeDtypeStruct(shape, BF) for shape in shapes],
        compiler_params=params,
    )(*operands, *[tile[0] for tile in tiles])


def call_flat(kernel, operands, tiles, shapes):
    arrays = []
    for array, _ in tiles:
        if all(array is not one for one in arrays):
            arrays.append(array)
    places = [([array is one for one in arrays].index(True), which) for array, which in tiles]
    count = len(operands)

    def body(*refs):
        held = refs[count : count + len(arrays)]
        views = [held[i].at[pl.ds(which, 1)] for i, which in places]
        kernel(*refs[:count], *views, *refs[count + len(arrays) :])

    return pl.pallas_call(
        body,
        out_shape=[jax.ShapeDtypeStruct(shape, BF) for shape in shapes],
        compiler_params=PARAMS,
    )(*operands, *arrays)


def tiled(R, C):
    def xor_row(value, step):
        return lax.ppermute(value, ROW, [(i, i ^ step) for i in range(R)])

    def xor_col(value, step):
        return lax.ppermute(value, "col", [(i, i ^ step) for i in range(C)])

    def in_plane(value):
        return [value] + [xor_row(value, step) for step in range(2, R, 2)]

    def with_mates(evens):
        return [block for even in evens for block in (even, xor_row(even, 1))]

    def shards(factor_rows, solved, inverses, link_tile, right_side):
        nrhs = solved.shape[0]
        group = nrhs // R
        rows = right_side.shape[1]
        size = inverses.shape[1]
        order = rows * C
        cut = (2 * group, rows)

        (pair,) = call(pack_kernel, [inverses, link_tile], [], [(2, size, rows)], WIDE)
        held = solved
        held, *_ = lax.optimization_barrier((held, pair))
        part = pl.pallas_call(
            panel_kernel,
            in_specs=[pl.BlockSpec(memory_space=pl.ANY)] * 2,
            out_shape=jax.ShapeDtypeStruct((R, C) + cut, BF),
            scratch_shapes=[
                pltpu.VMEM(solved.shape, BF),
                pltpu.VMEM(factor_rows.shape, BF),
                pltpu.SemaphoreType.DMA((5,)),
            ],
            compiler_params=WIDE,
        )(held, factor_rows)
        far = xor_col(pair, 2)
        evens = in_plane(inverses)
        part, *_ = lax.optimization_barrier((part, far, *evens))
        panel = exchange(part.reshape((R * C,) + cut), ROW + ("col",))
        mine = lax.dynamic_slice_in_dim(right_side, lax.axis_index(ROW) * group, group, 2)
        mine = mine.transpose(0, 2, 1).reshape(cut)

        own = with_mates(evens)
        first_tiles = [(tile, 0) for tile in own]
        (both,) = call(stack_kernel, [pair, far], [], [(3, size, rows)])
        wide = order // 2
        summed = (2 * group, wide)
        (sent,) = call(first_kernel, [mine, panel], first_tiles, [(2 * group, wide + rows // 2)])
        evens = in_plane(both)
        arrived = xor_col(sent, 2)
        side = jnp.stack([sent[:, wide:], arrived[:, wide:]])
        sent = (sent[:, :wide].astype(F32) + arrived[:, :wide].astype(F32)).astype(BF)
        other = xor_col(sent, 1)
        mates = []
        for even in evens:
            even, _ = lax.optimization_barrier((even, sent))
            mates.append(xor_row(even, 1))
        pairs = [block for one in zip(evens, mates) for block in one]
        last_tiles = [(tile, 1) for tile in own] + [(tile, 1) for tile in pairs]
        links = [(tile, i) for i in (0, 2) for tile in pairs]
        link = functools.partial(link_kernel, R)
        sent, first = call_flat(link, [sent, other, side], links + last_tiles, [summed, (group, order)])
        turn = functools.partial(turn_kernel, R)
        sent, short = call_flat(turn, [sent, xor_col(sent, 1)], last_tiles + links, [summed, (group, rows)])
        (sent,) = call_flat(last_kernel, [first, short, sent, xor_col(sent, 1)], first_tiles, [(R // 2 * C,) + cut])
        whole = exchange(sent, ("chip", "col"))
        remaining, back = pl.pallas_call(
            functools.partial(closing_kernel, C),
            out_shape=(
                jax.ShapeDtypeStruct(solved.shape, F32),
                jax.ShapeDtypeStruct((2, nrhs, rows), F32),
            ),
            compiler_params=PARAMS,
        )(solved, factor_rows, whole, xor_row(whole, 1))
        return (back.transpose(0, 2, 1), remaining)

    return shards


def solution(mesh):
    R, C = mesh.shape["row"], mesh.shape["col"]

    def whole(factor_rows, solved, inverses, link_tile, right_side):
        group, size, rows = solved.shape[0] // R, inverses.shape[1] // R, inverses.shape[2] // C
        if group == 8 and size % 128 == 0 and rows % 256 == 0 and C == 4 and R % 2 == 0:
            split, row, build = Mesh(mesh.devices.reshape(R // 2, 2, C), ROW + ("col",)), ROW, tiled
        else:
            split, row, build = mesh, ("row",), generic
        both = row + ("col",)
        placed = (P(None, None, both), P(None, both), P(None, row, "col"), P("col", row), P(None, "col", None))
        return jax.shard_map(
            build(R, C),
            mesh=split,
            in_specs=placed,
            out_specs=(P(None, "col", None), P(None, both)),
            check_vma=False,
        )(factor_rows, solved, inverses, link_tile, right_side)

    return whole
```

```python
import functools

import jax
import jax.numpy as jnp
from jax import lax
from jax.experimental import pallas as pl
from jax.experimental.pallas import tpu as pltpu
from jax.sharding import Mesh
from jax.sharding import PartitionSpec as P

BF = jnp.bfloat16
F32 = jnp.float32
ROW = ("chip", "core")
PARAMS = pltpu.CompilerParams(vmem_limit_bytes=12 * 2**20)
WIDE = pltpu.CompilerParams(vmem_limit_bytes=62 * 2**20)


def dot(left, right, contract):
    return lax.dot_general(left, right, ((contract[0], contract[1]), ((), ())), preferred_element_type=F32)


def plain(left, right):
    return dot(left, right, ((1,), (0,)))


def flipped(left, right):
    return dot(left, right, ((1,), (1,)))


def exchange(value, axes):
    return lax.all_to_all(value, axes, 0, 0, tiled=False)


def generic(R, C):
    def xor_row(value, step):
        return lax.ppermute(value, "row", [(i, i ^ step) for i in range(R)])

    def sum_over_col(part):
        sent = jnp.broadcast_to(part.astype(BF)[None], (C,) + part.shape)
        return jnp.sum(exchange(sent, "col").astype(F32), axis=0)

    def shards(factor_rows, solved, inverses, link_tile, right_side):
        nrhs = solved.shape[0]
        group = nrhs // R
        rows = right_side.shape[1]
        order = rows * C
        own = jnp.concatenate([inverses, link_tile.T[None]], axis=0)
        near = [own] + [xor_row(own, step) for step in range(2, R, 2)]
        near = jnp.stack(near, axis=1)
        mate = xor_row(near, 1)
        weights = jnp.concatenate([near, mate], axis=1).reshape(3, order, rows)
        first_tile, last_tile, link_back = weights[0], weights[1], weights[2]

        part = jnp.einsum("nc,kic->nki", solved, factor_rows, preferred_element_type=F32).astype(BF)
        part = part.reshape(R, group, 2, C, rows).transpose(0, 3, 2, 1, 4).reshape(R * C, 2 * group, rows)
        panel = jnp.sum(exchange(part, ("row", "col")).astype(F32), axis=0).reshape(2, group, rows)
        mine = lax.dynamic_slice_in_dim(right_side, lax.axis_index("row") * group, group, 2)
        residue = mine.transpose(0, 2, 1) - panel

        first_solved = sum_over_col(flipped(residue[0].astype(BF), first_tile)).astype(BF)
        residue_last = (residue[1] - plain(first_solved, link_back)).astype(BF)
        last_solved = sum_over_col(flipped(residue_last, last_tile)).astype(BF)
        last_short = plain(last_solved, last_tile).astype(BF)
        back_term = sum_over_col(flipped(last_short, link_back))
        carry = (first_solved.astype(F32) - back_term).astype(BF)
        first_short = plain(carry, first_tile).astype(BF)

        both = jnp.concatenate([first_short, last_short], axis=0)
        sent = jnp.broadcast_to(both[None], (R * C,) + both.shape)
        whole = exchange(sent, ("row", "col")).reshape(R, C, 2, group, rows)
        whole = whole.transpose(2, 0, 3, 1, 4).reshape(2, nrhs, order)
        return finish(factor_rows, solved, (whole[0], whole[1]), rows)

    return shards


def finish(factor_rows, solved, both, rows):
    update = plain(both[0], factor_rows[0]) + plain(both[1], factor_rows[1])
    remaining = solved.astype(F32) - update
    here = [lax.dynamic_slice_in_dim(one, lax.axis_index("col") * rows, rows, 1) for one in both]
    return (jnp.stack([one.astype(F32).T for one in here]), remaining)


def fold(value):
    half = value.shape[-1] // 2
    return jnp.concatenate([value[..., :half], value[..., half:]], axis=-2)


def unfold(value):
    half = value.shape[-2] // 2
    return jnp.concatenate([value[..., :half, :], value[..., half:, :]], axis=-1)


def pack_kernel(inv_ref, link_ref, pair_ref):
    pair_ref[0] = inv_ref[1]
    pair_ref[1] = link_ref[...].T


def stack_kernel(own_ref, far_ref, both_ref):
    both_ref[0] = own_ref[1]
    both_ref[1:] = far_ref[...]


def panel_kernel(solved_ref, factor_ref, part_ref, solved, factor, sems):
    R, C, double, rows = part_ref.shape
    step = C // 4
    copies = [pltpu.make_async_copy(solved_ref, solved, sems.at[0])]
    for i in range(4):
        chunk = pl.ds(i * step * rows, step * rows)
        copies.append(pltpu.make_async_copy(factor_ref.at[:, chunk], factor.at[:, chunk], sems.at[1 + i]))
    for copy in copies:
        copy.start()
    copies[0].wait()
    value = solved[...]
    for c in range(C):
        if c % step == 0:
            copies[1 + c // step].wait()
        halves = [flipped(value, factor[k, c * rows : (c + 1) * rows]) for k in range(2)]
        halves = [half.reshape(R, double // 2, rows) for half in halves]
        part_ref[:, c] = jnp.concatenate(halves, axis=1).astype(BF)


def closing_kernel(C, solved_ref, factor_ref, own_ref, other_ref, remaining_ref, back_ref):
    chips = own_ref.shape[0] // C
    group, rows = own_ref.shape[1] // 2, own_ref.shape[2]
    even = lax.axis_index("core") == 0
    here = lax.axis_index("col")

    def columns(k, c):
        parts = []
        for chip in range(chips):
            own = own_ref[chip * C + c, k * group : (k + 1) * group].astype(F32)
            other = other_ref[chip * C + c, k * group : (k + 1) * group].astype(F32)
            parts += [jnp.where(even, own, other), jnp.where(even, other, own)]
        return jnp.concatenate(parts, axis=0)

    update = None
    for k in range(2):
        back_ref[k] = columns(k, here)
        whole = jnp.concatenate([columns(k, c).astype(BF) for c in range(C)], axis=1)
        term = plain(whole, factor_ref[k])
        update = term if update is None else update + term
    remaining_ref[...] = solved_ref[...].astype(F32) - update


def stacked(tiles):
    return jnp.concatenate([tile[0] for tile in tiles], axis=0)


def across(value, tiles):
    return flipped(value, stacked(tiles))


def along(value, tiles):
    return plain(value, stacked(tiles))


def first_kernel(side_ref, panel_ref, *refs):
    tiles, sent_ref = refs[:-1], refs[-1]
    group = side_ref.shape[0] // 2
    total = panel_ref[0].astype(F32)
    for i in range(1, panel_ref.shape[0]):
        total += panel_ref[i].astype(F32)
    residue = side_ref[...] - total
    solved = across(residue[:group].astype(BF), tiles)
    sent_ref[...] = jnp.concatenate([fold(solved), fold(residue[group:])], axis=1).astype(BF)


def pair_sum(own_ref, other_ref):
    return unfold(own_ref[...].astype(F32) + other_ref[...].astype(F32))


def link_kernel(near, own_ref, other_ref, side_ref, *refs):
    links, last_tiles = refs[: 2 * near], refs[2 * near : 4 * near]
    sent_ref, first_ref = refs[4 * near :]
    first = pair_sum(own_ref, other_ref).astype(BF)
    first_ref[...] = first
    total = None
    for j in range(2):
        residue = unfold(side_ref[j].astype(F32)) - along(first, links[j * near : (j + 1) * near])
        term = across(residue.astype(BF), last_tiles[j * near : (j + 1) * near])
        total = term if total is None else total + term
    sent_ref[...] = fold(total).astype(BF)


def turn_kernel(near, own_ref, other_ref, *refs):
    last_tiles, links = refs[: 2 * near], refs[2 * near : 4 * near]
    sent_ref, short_ref = refs[4 * near :]
    last = pair_sum(own_ref, other_ref).astype(BF)
    total = None
    for j in range(2):
        short = along(last, last_tiles[j * near : (j + 1) * near]).astype(BF)
        if j == 0:
            short_ref[...] = short
        term = across(short, links[j * near : (j + 1) * near])
        total = term if total is None else total + term
    sent_ref[...] = fold(total).astype(BF)


def last_kernel(first_ref, short_ref, own_ref, other_ref, *refs):
    tiles, sent_ref = refs[:-1], refs[-1]
    carry = (first_ref[...].astype(F32) - pair_sum(own_ref, other_ref)).astype(BF)
    both = jnp.concatenate([along(carry, tiles), short_ref[...].astype(F32)], axis=0).astype(BF)
    for i in range(sent_ref.shape[0]):
        sent_ref[i] = both


def whole_spec(shape):
    return pl.BlockSpec(shape, lambda i: (0,) * len(shape))


def call(kernel, operands, tiles, shapes, params=PARAMS):
    def tile_spec(array, which):
        return pl.BlockSpec((1,) + array.shape[1:], lambda i: (which, 0, 0))

    return pl.pallas_call(
        kernel,
        grid=(1,),
        in_specs=[whole_spec(one.shape) for one in operands] + [tile_spec(*tile) for tile in tiles],
        out_specs=[whole_spec(shape) for shape in shapes],
        out_shape=[jax.ShapeDtypeStruct(shape, BF) for shape in shapes],
        compiler_params=params,
    )(*operands, *[tile[0] for tile in tiles])


def call_flat(kernel, operands, tiles, shapes):
    arrays = []
    for array, _ in tiles:
        if all(array is not one for one in arrays):
            arrays.append(array)
    places = [([array is one for one in arrays].index(True), which) for array, which in tiles]
    count = len(operands)

    def body(*refs):
        held = refs[count : count + len(arrays)]
        views = [held[i].at[pl.ds(which, 1)] for i, which in places]
        kernel(*refs[:count], *views, *refs[count + len(arrays) :])

    return pl.pallas_call(
        body,
        out_shape=[jax.ShapeDtypeStruct(shape, BF) for shape in shapes],
        compiler_params=PARAMS,
    )(*operands, *arrays)


def tiled(R, C):
    def xor_row(value, step):
        return lax.ppermute(value, ROW, [(i, i ^ step) for i in range(R)])

    def xor_col(value, step):
        return lax.ppermute(value, "col", [(i, i ^ step) for i in range(C)])

    def in_plane(value):
        return [value] + [xor_row(value, step) for step in range(2, R, 2)]

    def with_mates(evens):
        return [block for even in evens for block in (even, xor_row(even, 1))]

    def shards(factor_rows, solved, inverses, link_tile, right_side):
        nrhs = solved.shape[0]
        group = nrhs // R
        rows = right_side.shape[1]
        size = inverses.shape[1]
        order = rows * C
        cut = (2 * group, rows)

        (pair,) = call(pack_kernel, [inverses, link_tile], [], [(2, size, rows)], WIDE)
        held = solved
        held, *_ = lax.optimization_barrier((held, pair))
        part = pl.pallas_call(
            panel_kernel,
            in_specs=[pl.BlockSpec(memory_space=pl.ANY)] * 2,
            out_shape=jax.ShapeDtypeStruct((R, C) + cut, BF),
            scratch_shapes=[
                pltpu.VMEM(solved.shape, BF),
                pltpu.VMEM(factor_rows.shape, BF),
                pltpu.SemaphoreType.DMA((5,)),
            ],
            compiler_params=WIDE,
        )(held, factor_rows)
        far = xor_col(pair, 2)
        evens = in_plane(inverses)
        part, *_ = lax.optimization_barrier((part, far, *evens))
        panel = exchange(part.reshape((R * C,) + cut), ROW + ("col",))
        mine = lax.dynamic_slice_in_dim(right_side, lax.axis_index(ROW) * group, group, 2)
        mine = mine.transpose(0, 2, 1).reshape(cut)

        own = with_mates(evens)
        first_tiles = [(tile, 0) for tile in own]
        (both,) = call(stack_kernel, [pair, far], [], [(3, size, rows)])
        wide = order // 2
        summed = (2 * group, wide)
        (sent,) = call(first_kernel, [mine, panel], first_tiles, [(2 * group, wide + rows // 2)])
        evens = in_plane(both)
        arrived = xor_col(sent, 2)
        side = jnp.stack([sent[:, wide:], arrived[:, wide:]])
        sent = (sent[:, :wide].astype(F32) + arrived[:, :wide].astype(F32)).astype(BF)
        other = xor_col(sent, 1)
        mates = []
        for even in evens:
            even, _ = lax.optimization_barrier((even, sent))
            mates.append(xor_row(even, 1))
        pairs = [block for one in zip(evens, mates) for block in one]
        last_tiles = [(tile, 1) for tile in own] + [(tile, 1) for tile in pairs]
        links = [(tile, i) for i in (0, 2) for tile in pairs]
        link = functools.partial(link_kernel, R)
        sent, first = call_flat(link, [sent, other, side], links + last_tiles, [summed, (group, order)])
        turn = functools.partial(turn_kernel, R)
        sent, short = call_flat(turn, [sent, xor_col(sent, 1)], last_tiles + links, [summed, (group, rows)])
        (sent,) = call_flat(last_kernel, [first, short, sent, xor_col(sent, 1)], first_tiles, [(R // 2 * C,) + cut])
        whole = exchange(sent, ("chip", "col"))
        remaining, back = pl.pallas_call(
            functools.partial(closing_kernel, C),
            out_shape=(
                jax.ShapeDtypeStruct(solved.shape, F32),
                jax.ShapeDtypeStruct((2, nrhs, rows), F32),
            ),
            compiler_params=PARAMS,
        )(solved, factor_rows, whole, xor_row(whole, 1))
        return (back.transpose(0, 2, 1), remaining)

    return shards


def solution(mesh):
    R, C = mesh.shape["row"], mesh.shape["col"]

    def whole(factor_rows, solved, inverses, link_tile, right_side):
        group, size, rows = solved.shape[0] // R, inverses.shape[1] // R, inverses.shape[2] // C
        if group == 8 and size % 128 == 0 and rows % 256 == 0 and C == 4 and R % 2 == 0:
            split, row, build = Mesh(mesh.devices.reshape(R // 2, 2, C), ROW + ("col",)), ROW, tiled
        else:
            split, row, build = mesh, ("row",), generic
        both = row + ("col",)
        placed = (P(None, None, both), P(None, both), P(None, row, "col"), P("col", row), P(None, "col", None))
        return jax.shard_map(
            build(R, C),
            mesh=split,
            in_specs=placed,
            out_specs=(P(None, "col", None), P(None, both)),
            check_vma=False,
        )(factor_rows, solved, inverses, link_tile, right_side)

    return whole
```

```python
import functools

import jax
import jax.numpy as jnp
from jax import lax
from jax.experimental import pallas as pl
from jax.experimental.pallas import tpu as pltpu
from jax.sharding import Mesh
from jax.sharding import PartitionSpec as P

BF = jnp.bfloat16
F32 = jnp.float32
ROW = ("chip", "core")
PARAMS = pltpu.CompilerParams(vmem_limit_bytes=12 * 2**20)
WIDE = pltpu.CompilerParams(vmem_limit_bytes=62 * 2**20)


def dot(left, right, contract):
    return lax.dot_general(left, right, ((contract[0], contract[1]), ((), ())), preferred_element_type=F32)


def plain(left, right):
    return dot(left, right, ((1,), (0,)))


def flipped(left, right):
    return dot(left, right, ((1,), (1,)))


def exchange(value, axes):
    return lax.all_to_all(value, axes, 0, 0, tiled=False)


def generic(R, C):
    def xor_row(value, step):
        return lax.ppermute(value, "row", [(i, i ^ step) for i in range(R)])

    def sum_over_col(part):
        sent = jnp.broadcast_to(part.astype(BF)[None], (C,) + part.shape)
        return jnp.sum(exchange(sent, "col").astype(F32), axis=0)

    def shards(factor_rows, solved, inverses, link_tile, right_side):
        nrhs = solved.shape[0]
        group = nrhs // R
        rows = right_side.shape[1]
        order = rows * C
        own = jnp.concatenate([inverses, link_tile.T[None]], axis=0)
        near = [own] + [xor_row(own, step) for step in range(2, R, 2)]
        near = jnp.stack(near, axis=1)
        mate = xor_row(near, 1)
        weights = jnp.concatenate([near, mate], axis=1).reshape(3, order, rows)
        first_tile, last_tile, link_back = weights[0], weights[1], weights[2]

        part = jnp.einsum("nc,kic->nki", solved, factor_rows, preferred_element_type=F32).astype(BF)
        part = part.reshape(R, group, 2, C, rows).transpose(0, 3, 2, 1, 4).reshape(R * C, 2 * group, rows)
        panel = jnp.sum(exchange(part, ("row", "col")).astype(F32), axis=0).reshape(2, group, rows)
        mine = lax.dynamic_slice_in_dim(right_side, lax.axis_index("row") * group, group, 2)
        residue = mine.transpose(0, 2, 1) - panel

        first_solved = sum_over_col(flipped(residue[0].astype(BF), first_tile)).astype(BF)
        residue_last = (residue[1] - plain(first_solved, link_back)).astype(BF)
        last_solved = sum_over_col(flipped(residue_last, last_tile)).astype(BF)
        last_short = plain(last_solved, last_tile).astype(BF)
        back_term = sum_over_col(flipped(last_short, link_back))
        carry = (first_solved.astype(F32) - back_term).astype(BF)
        first_short = plain(carry, first_tile).astype(BF)

        both = jnp.concatenate([first_short, last_short], axis=0)
        sent = jnp.broadcast_to(both[None], (R * C,) + both.shape)
        whole = exchange(sent, ("row", "col")).reshape(R, C, 2, group, rows)
        whole = whole.transpose(2, 0, 3, 1, 4).reshape(2, nrhs, order)
        return finish(factor_rows, solved, (whole[0], whole[1]), rows)

    return shards


def finish(factor_rows, solved, both, rows):
    update = plain(both[0], factor_rows[0]) + plain(both[1], factor_rows[1])
    remaining = solved.astype(F32) - update
    here = [lax.dynamic_slice_in_dim(one, lax.axis_index("col") * rows, rows, 1) for one in both]
    return (jnp.stack([one.astype(F32).T for one in here]), remaining)


def fold(value):
    half = value.shape[-1] // 2
    return jnp.concatenate([value[..., :half], value[..., half:]], axis=-2)


def unfold(value):
    half = value.shape[-2] // 2
    return jnp.concatenate([value[..., :half, :], value[..., half:, :]], axis=-1)


def pack_kernel(inv_ref, link_ref, pair_ref):
    pair_ref[0] = inv_ref[1]
    pair_ref[1] = link_ref[...].T


def stack_kernel(own_ref, far_ref, both_ref):
    both_ref[0] = own_ref[1]
    both_ref[1:] = far_ref[...]


def panel_kernel(solved_ref, factor_ref, part_ref, solved, factor, sems):
    R, C, double, rows = part_ref.shape
    step = C // 2
    copies = [pltpu.make_async_copy(solved_ref, solved, sems.at[0])]
    for i in range(2):
        chunk = pl.ds(i * step * rows, step * rows)
        copies.append(pltpu.make_async_copy(factor_ref.at[:, chunk], factor.at[:, chunk], sems.at[1 + i]))
    for copy in copies:
        copy.start()
    copies[0].wait()
    value = solved[...]
    for c in range(C):
        if c % step == 0:
            copies[1 + c // step].wait()
        halves = [flipped(value, factor[k, c * rows : (c + 1) * rows]) for k in range(2)]
        halves = [half.reshape(R, double // 2, rows) for half in halves]
        part_ref[:, c] = jnp.concatenate(halves, axis=1).astype(BF)


def closing_kernel(C, solved_ref, factor_ref, own_ref, other_ref, remaining_ref, back_ref):
    chips = own_ref.shape[0] // C
    group, rows = own_ref.shape[1] // 2, own_ref.shape[2]
    even = lax.axis_index("core") == 0
    here = lax.axis_index("col")

    def columns(k, c):
        parts = []
        for chip in range(chips):
            own = own_ref[chip * C + c, k * group : (k + 1) * group].astype(F32)
            other = other_ref[chip * C + c, k * group : (k + 1) * group].astype(F32)
            parts += [jnp.where(even, own, other), jnp.where(even, other, own)]
        return jnp.concatenate(parts, axis=0)

    update = None
    for k in range(2):
        back_ref[k] = columns(k, here)
        for c in range(C):
            term = plain(columns(k, c).astype(BF), factor_ref[k, c * rows : (c + 1) * rows])
            update = term if update is None else update + term
    remaining_ref[...] = solved_ref[...].astype(F32) - update


def stacked(tiles):
    return jnp.concatenate([tile[0] for tile in tiles], axis=0)


def across(value, tiles):
    return flipped(value, stacked(tiles))


def along(value, tiles):
    return plain(value, stacked(tiles))


def first_kernel(side_ref, panel_ref, *refs):
    tiles, sent_ref = refs[:-1], refs[-1]
    group = side_ref.shape[0] // 2
    total = panel_ref[0].astype(F32)
    for i in range(1, panel_ref.shape[0]):
        total += panel_ref[i].astype(F32)
    residue = side_ref[...] - total
    solved = across(residue[:group].astype(BF), tiles)
    sent_ref[...] = jnp.concatenate([fold(solved), fold(residue[group:])], axis=1).astype(BF)


def pair_sum(own_ref, other_ref):
    return unfold(own_ref[...].astype(F32) + other_ref[...].astype(F32))


def link_kernel(near, own_ref, other_ref, side_ref, *refs):
    links, last_tiles = refs[: 2 * near], refs[2 * near : 4 * near]
    sent_ref, first_ref = refs[4 * near :]
    first = pair_sum(own_ref, other_ref).astype(BF)
    first_ref[...] = first
    total = None
    for j in range(2):
        residue = unfold(side_ref[j].astype(F32)) - along(first, links[j * near : (j + 1) * near])
        term = across(residue.astype(BF), last_tiles[j * near : (j + 1) * near])
        total = term if total is None else total + term
    sent_ref[...] = fold(total).astype(BF)


def turn_kernel(near, own_ref, other_ref, *refs):
    last_tiles, links = refs[: 2 * near], refs[2 * near : 4 * near]
    sent_ref, short_ref = refs[4 * near :]
    last = pair_sum(own_ref, other_ref).astype(BF)
    total = None
    for j in range(2):
        short = along(last, last_tiles[j * near : (j + 1) * near]).astype(BF)
        if j == 0:
            short_ref[...] = short
        term = across(short, links[j * near : (j + 1) * near])
        total = term if total is None else total + term
    sent_ref[...] = fold(total).astype(BF)


def last_kernel(first_ref, short_ref, own_ref, other_ref, *refs):
    tiles, sent_ref = refs[:-1], refs[-1]
    carry = (first_ref[...].astype(F32) - pair_sum(own_ref, other_ref)).astype(BF)
    both = jnp.concatenate([along(carry, tiles), short_ref[...].astype(F32)], axis=0).astype(BF)
    for i in range(sent_ref.shape[0]):
        sent_ref[i] = both


def whole_spec(shape):
    return pl.BlockSpec(shape, lambda i: (0,) * len(shape))


def call(kernel, operands, tiles, shapes, params=PARAMS):
    def tile_spec(array, which):
        return pl.BlockSpec((1,) + array.shape[1:], lambda i: (which, 0, 0))

    return pl.pallas_call(
        kernel,
        grid=(1,),
        in_specs=[whole_spec(one.shape) for one in operands] + [tile_spec(*tile) for tile in tiles],
        out_specs=[whole_spec(shape) for shape in shapes],
        out_shape=[jax.ShapeDtypeStruct(shape, BF) for shape in shapes],
        compiler_params=params,
    )(*operands, *[tile[0] for tile in tiles])


def call_flat(kernel, operands, tiles, shapes):
    arrays = []
    for array, _ in tiles:
        if all(array is not one for one in arrays):
            arrays.append(array)
    places = [([array is one for one in arrays].index(True), which) for array, which in tiles]
    count = len(operands)

    def body(*refs):
        held = refs[count : count + len(arrays)]
        views = [held[i].at[pl.ds(which, 1)] for i, which in places]
        kernel(*refs[:count], *views, *refs[count + len(arrays) :])

    return pl.pallas_call(
        body,
        out_shape=[jax.ShapeDtypeStruct(shape, BF) for shape in shapes],
        compiler_params=PARAMS,
    )(*operands, *arrays)


def tiled(R, C):
    def xor_row(value, step):
        return lax.ppermute(value, ROW, [(i, i ^ step) for i in range(R)])

    def xor_col(value, step):
        return lax.ppermute(value, "col", [(i, i ^ step) for i in range(C)])

    def in_plane(value):
        return [value] + [xor_row(value, step) for step in range(2, R, 2)]

    def with_mates(evens):
        return [block for even in evens for block in (even, xor_row(even, 1))]

    def shards(factor_rows, solved, inverses, link_tile, right_side):
        nrhs = solved.shape[0]
        group = nrhs // R
        rows = right_side.shape[1]
        size = inverses.shape[1]
        order = rows * C
        cut = (2 * group, rows)

        (pair,) = call(pack_kernel, [inverses, link_tile], [], [(2, size, rows)], WIDE)
        held = solved
        held, *_ = lax.optimization_barrier((held, pair))
        part = pl.pallas_call(
            panel_kernel,
            in_specs=[pl.BlockSpec(memory_space=pl.ANY)] * 2,
            out_shape=jax.ShapeDtypeStruct((R, C) + cut, BF),
            scratch_shapes=[
                pltpu.VMEM(solved.shape, BF),
                pltpu.VMEM(factor_rows.shape, BF),
                pltpu.SemaphoreType.DMA((3,)),
            ],
            compiler_params=WIDE,
        )(held, factor_rows)
        far = xor_col(pair, 2)
        evens = in_plane(inverses)
        part, *_ = lax.optimization_barrier((part, far, *evens))
        panel = exchange(part.reshape((R * C,) + cut), ROW + ("col",))
        mine = lax.dynamic_slice_in_dim(right_side, lax.axis_index(ROW) * group, group, 2)
        mine = mine.transpose(0, 2, 1).reshape(cut)

        own = with_mates(evens)
        first_tiles = [(tile, 0) for tile in own]
        (both,) = call(stack_kernel, [pair, far], [], [(3, size, rows)])
        wide = order // 2
        summed = (2 * group, wide)
        (sent,) = call(first_kernel, [mine, panel], first_tiles, [(2 * group, wide + rows // 2)])
        evens = in_plane(both)
        arrived = xor_col(sent, 2)
        side = jnp.stack([sent[:, wide:], arrived[:, wide:]])
        sent = (sent[:, :wide].astype(F32) + arrived[:, :wide].astype(F32)).astype(BF)
        other = xor_col(sent, 1)
        mates = []
        for even in evens:
            even, _ = lax.optimization_barrier((even, sent))
            mates.append(xor_row(even, 1))
        pairs = [block for one in zip(evens, mates) for block in one]
        last_tiles = [(tile, 1) for tile in own] + [(tile, 1) for tile in pairs]
        links = [(tile, i) for i in (0, 2) for tile in pairs]
        link = functools.partial(link_kernel, R)
        sent, first = call_flat(link, [sent, other, side], links + last_tiles, [summed, (group, order)])
        turn = functools.partial(turn_kernel, R)
        sent, short = call_flat(turn, [sent, xor_col(sent, 1)], last_tiles + links, [summed, (group, rows)])
        (sent,) = call_flat(last_kernel, [first, short, sent, xor_col(sent, 1)], first_tiles, [(R // 2 * C,) + cut])
        whole = exchange(sent, ("chip", "col"))
        remaining, back = pl.pallas_call(
            functools.partial(closing_kernel, C),
            out_shape=(
                jax.ShapeDtypeStruct(solved.shape, F32),
                jax.ShapeDtypeStruct((2, nrhs, rows), F32),
            ),
            compiler_params=PARAMS,
        )(solved, factor_rows, whole, xor_row(whole, 1))
        return (back.transpose(0, 2, 1), remaining)

    return shards


def solution(mesh):
    R, C = mesh.shape["row"], mesh.shape["col"]

    def whole(factor_rows, solved, inverses, link_tile, right_side):
        group, size, rows = solved.shape[0] // R, inverses.shape[1] // R, inverses.shape[2] // C
        if group == 8 and size % 128 == 0 and rows % 256 == 0 and C == 4 and R % 2 == 0:
            split, row, build = Mesh(mesh.devices.reshape(R // 2, 2, C), ROW + ("col",)), ROW, tiled
        else:
            split, row, build = mesh, ("row",), generic
        both = row + ("col",)
        placed = (P(None, None, both), P(None, both), P(None, row, "col"), P("col", row), P(None, "col", None))
        return jax.shard_map(
            build(R, C),
            mesh=split,
            in_specs=placed,
            out_specs=(P(None, "col", None), P(None, both)),
            check_vma=False,
        )(factor_rows, solved, inverses, link_tile, right_side)

    return whole
```

```python
import functools

import jax
import jax.numpy as jnp
from jax import lax
from jax.experimental import pallas as pl
from jax.experimental.pallas import tpu as pltpu
from jax.sharding import Mesh
from jax.sharding import PartitionSpec as P

BF = jnp.bfloat16
F32 = jnp.float32
ROW = ("chip", "core")
PARAMS = pltpu.CompilerParams(vmem_limit_bytes=12 * 2**20)
WIDE = pltpu.CompilerParams(vmem_limit_bytes=62 * 2**20)


def dot(left, right, contract):
    return lax.dot_general(left, right, ((contract[0], contract[1]), ((), ())), preferred_element_type=F32)


def plain(left, right):
    return dot(left, right, ((1,), (0,)))


def flipped(left, right):
    return dot(left, right, ((1,), (1,)))


def exchange(value, axes):
    return lax.all_to_all(value, axes, 0, 0, tiled=False)


def generic(R, C):
    def xor_row(value, step):
        return lax.ppermute(value, "row", [(i, i ^ step) for i in range(R)])

    def sum_over_col(part):
        sent = jnp.broadcast_to(part.astype(BF)[None], (C,) + part.shape)
        return jnp.sum(exchange(sent, "col").astype(F32), axis=0)

    def shards(factor_rows, solved, inverses, link_tile, right_side):
        nrhs = solved.shape[0]
        group = nrhs // R
        rows = right_side.shape[1]
        order = rows * C
        own = jnp.concatenate([inverses, link_tile.T[None]], axis=0)
        near = [own] + [xor_row(own, step) for step in range(2, R, 2)]
        near = jnp.stack(near, axis=1)
        mate = xor_row(near, 1)
        weights = jnp.concatenate([near, mate], axis=1).reshape(3, order, rows)
        first_tile, last_tile, link_back = weights[0], weights[1], weights[2]

        part = jnp.einsum("nc,kic->nki", solved, factor_rows, preferred_element_type=F32).astype(BF)
        part = part.reshape(R, group, 2, C, rows).transpose(0, 3, 2, 1, 4).reshape(R * C, 2 * group, rows)
        panel = jnp.sum(exchange(part, ("row", "col")).astype(F32), axis=0).reshape(2, group, rows)
        mine = lax.dynamic_slice_in_dim(right_side, lax.axis_index("row") * group, group, 2)
        residue = mine.transpose(0, 2, 1) - panel

        first_solved = sum_over_col(flipped(residue[0].astype(BF), first_tile)).astype(BF)
        residue_last = (residue[1] - plain(first_solved, link_back)).astype(BF)
        last_solved = sum_over_col(flipped(residue_last, last_tile)).astype(BF)
        last_short = plain(last_solved, last_tile).astype(BF)
        back_term = sum_over_col(flipped(last_short, link_back))
        carry = (first_solved.astype(F32) - back_term).astype(BF)
        first_short = plain(carry, first_tile).astype(BF)

        both = jnp.concatenate([first_short, last_short], axis=0)
        sent = jnp.broadcast_to(both[None], (R * C,) + both.shape)
        whole = exchange(sent, ("row", "col")).reshape(R, C, 2, group, rows)
        whole = whole.transpose(2, 0, 3, 1, 4).reshape(2, nrhs, order)
        return finish(factor_rows, solved, (whole[0], whole[1]), rows)

    return shards


def finish(factor_rows, solved, both, rows):
    update = plain(both[0], factor_rows[0]) + plain(both[1], factor_rows[1])
    remaining = solved.astype(F32) - update
    here = [lax.dynamic_slice_in_dim(one, lax.axis_index("col") * rows, rows, 1) for one in both]
    return (jnp.stack([one.astype(F32).T for one in here]), remaining)


def fold(value):
    half = value.shape[-1] // 2
    return jnp.concatenate([value[..., :half], value[..., half:]], axis=-2)


def unfold(value):
    half = value.shape[-2] // 2
    return jnp.concatenate([value[..., :half, :], value[..., half:, :]], axis=-1)


def pack_kernel(inv_ref, link_ref, pair_ref):
    pair_ref[0] = inv_ref[1]
    pair_ref[1] = link_ref[...].T


def stack_kernel(own_ref, far_ref, both_ref):
    both_ref[0] = own_ref[1]
    both_ref[1:] = far_ref[...]


def panel_kernel(solved_ref, factor_ref, part_ref, solved, factor, sems):
    R, C, double, rows = part_ref.shape
    step = C // 2
    copies = [pltpu.make_async_copy(solved_ref, solved, sems.at[0])]
    for i in range(2):
        chunk = pl.ds(i * step * rows, step * rows)
        copies.append(pltpu.make_async_copy(factor_ref.at[:, chunk], factor.at[:, chunk], sems.at[1 + i]))
    for copy in copies:
        copy.start()
    copies[0].wait()
    value = solved[...]
    for c in range(C):
        if c % step == 0:
            copies[1 + c // step].wait()
        halves = [flipped(value, factor[k, c * rows : (c + 1) * rows]) for k in range(2)]
        halves = [half.reshape(R, double // 2, rows) for half in halves]
        part_ref[:, c] = jnp.concatenate(halves, axis=1).astype(BF)


def closing_kernel(C, solved_ref, factor_ref, own_ref, other_ref, remaining_ref, back_ref):
    chips = own_ref.shape[0] // C
    group, rows = own_ref.shape[1] // 2, own_ref.shape[2]
    even = lax.axis_index("core") == 0
    here = lax.axis_index("col")

    def columns(k, c):
        parts = []
        for chip in range(chips):
            own = own_ref[chip * C + c, k * group : (k + 1) * group].astype(F32)
            other = other_ref[chip * C + c, k * group : (k + 1) * group].astype(F32)
            parts += [jnp.where(even, own, other), jnp.where(even, other, own)]
        return jnp.concatenate(parts, axis=0)

    update = None
    for k in range(2):
        back_ref[k] = columns(k, here)
        whole = jnp.concatenate([columns(k, c).astype(BF) for c in range(C)], axis=1)
        term = plain(whole, factor_ref[k])
        update = term if update is None else update + term
    remaining_ref[...] = solved_ref[...].astype(F32) - update


def stacked(tiles):
    return jnp.concatenate([tile[0] for tile in tiles], axis=0)


def across(value, tiles):
    return flipped(value, stacked(tiles))


def along(value, tiles):
    return plain(value, stacked(tiles))


def first_kernel(side_ref, panel_ref, *refs):
    tiles, sent_ref = refs[:-1], refs[-1]
    group = side_ref.shape[0] // 2
    total = panel_ref[0].astype(F32)
    for i in range(1, panel_ref.shape[0]):
        total += panel_ref[i].astype(F32)
    residue = side_ref[...] - total
    solved = across(residue[:group].astype(BF), tiles)
    sent_ref[...] = jnp.concatenate([fold(solved), fold(residue[group:])], axis=1).astype(BF)


def pair_sum(own_ref, other_ref):
    return unfold(own_ref[...].astype(F32) + other_ref[...].astype(F32))


def link_kernel(near, own_ref, other_ref, side_ref, *refs):
    links, last_tiles = refs[: 2 * near], refs[2 * near : 4 * near]
    sent_ref, first_ref = refs[4 * near :]
    first = pair_sum(own_ref, other_ref).astype(BF)
    first_ref[...] = first
    total = None
    for j in range(2):
        residue = unfold(side_ref[j].astype(F32)) - along(first, links[j * near : (j + 1) * near])
        term = across(residue.astype(BF), last_tiles[j * near : (j + 1) * near])
        total = term if total is None else total + term
    sent_ref[...] = fold(total).astype(BF)


def turn_kernel(near, own_ref, other_ref, *refs):
    last_tiles, links = refs[: 2 * near], refs[2 * near : 4 * near]
    sent_ref, short_ref = refs[4 * near :]
    last = pair_sum(own_ref, other_ref).astype(BF)
    total = None
    for j in range(2):
        short = along(last, last_tiles[j * near : (j + 1) * near]).astype(BF)
        if j == 0:
            short_ref[...] = short
        term = across(short, links[j * near : (j + 1) * near])
        total = term if total is None else total + term
    sent_ref[...] = fold(total).astype(BF)


def last_kernel(first_ref, short_ref, own_ref, other_ref, *refs):
    tiles, sent_ref = refs[:-1], refs[-1]
    carry = (first_ref[...].astype(F32) - pair_sum(own_ref, other_ref)).astype(BF)
    both = jnp.concatenate([along(carry, tiles), short_ref[...].astype(F32)], axis=0).astype(BF)
    for i in range(sent_ref.shape[0]):
        sent_ref[i] = both


def whole_spec(shape):
    return pl.BlockSpec(shape, lambda i: (0,) * len(shape))


def call(kernel, operands, tiles, shapes, params=PARAMS):
    def tile_spec(array, which):
        return pl.BlockSpec((1,) + array.shape[1:], lambda i: (which, 0, 0))

    return pl.pallas_call(
        kernel,
        grid=(1,),
        in_specs=[whole_spec(one.shape) for one in operands] + [tile_spec(*tile) for tile in tiles],
        out_specs=[whole_spec(shape) for shape in shapes],
        out_shape=[jax.ShapeDtypeStruct(shape, BF) for shape in shapes],
        compiler_params=params,
    )(*operands, *[tile[0] for tile in tiles])


def call_flat(kernel, operands, tiles, shapes):
    arrays = []
    for array, _ in tiles:
        if all(array is not one for one in arrays):
            arrays.append(array)
    places = [([array is one for one in arrays].index(True), which) for array, which in tiles]
    count = len(operands)

    def body(*refs):
        held = refs[count : count + len(arrays)]
        views = [held[i].at[pl.ds(which, 1)] for i, which in places]
        kernel(*refs[:count], *views, *refs[count + len(arrays) :])

    return pl.pallas_call(
        body,
        out_shape=[jax.ShapeDtypeStruct(shape, BF) for shape in shapes],
        compiler_params=PARAMS,
    )(*operands, *arrays)


def tiled(R, C):
    def xor_row(value, step):
        return lax.ppermute(value, ROW, [(i, i ^ step) for i in range(R)])

    def xor_col(value, step):
        return lax.ppermute(value, "col", [(i, i ^ step) for i in range(C)])

    def in_plane(value):
        return [value] + [xor_row(value, step) for step in range(2, R, 2)]

    def with_mates(evens):
        return [block for even in evens for block in (even, xor_row(even, 1))]

    def shards(factor_rows, solved, inverses, link_tile, right_side):
        nrhs = solved.shape[0]
        group = nrhs // R
        rows = right_side.shape[1]
        size = inverses.shape[1]
        order = rows * C
        cut = (2 * group, rows)

        (pair,) = call(pack_kernel, [inverses, link_tile], [], [(2, size, rows)], WIDE)
        held = solved
        held, *_ = lax.optimization_barrier((held, pair))
        part = pl.pallas_call(
            panel_kernel,
            in_specs=[pl.BlockSpec(memory_space=pl.ANY)] * 2,
            out_shape=jax.ShapeDtypeStruct((R, C) + cut, BF),
            scratch_shapes=[
                pltpu.VMEM(solved.shape, BF),
                pltpu.VMEM(factor_rows.shape, BF),
                pltpu.SemaphoreType.DMA((3,)),
            ],
            compiler_params=WIDE,
        )(held, factor_rows)
        far = xor_col(pair, 2)
        evens = in_plane(inverses)
        part, *_ = lax.optimization_barrier((part, far, *evens))
        panel = exchange(part.reshape((R * C,) + cut), ROW + ("col",))
        mine = lax.dynamic_slice_in_dim(right_side, lax.axis_index(ROW) * group, group, 2)
        mine = mine.transpose(0, 2, 1).reshape(cut)

        own = with_mates(evens)
        first_tiles = [(tile, 0) for tile in own]
        (both,) = call(stack_kernel, [pair, far], [], [(3, size, rows)])
        wide = order // 2
        summed = (2 * group, wide)
        (sent,) = call(first_kernel, [mine, panel], first_tiles, [(2 * group, wide + rows // 2)])
        evens = in_plane(both)
        arrived = xor_col(sent, 2)
        side = jnp.stack([sent[:, wide:], arrived[:, wide:]])
        sent = (sent[:, :wide].astype(F32) + arrived[:, :wide].astype(F32)).astype(BF)
        other = xor_col(sent, 1)
        mates = []
        for even in evens:
            even, _ = lax.optimization_barrier((even, sent))
            mates.append(xor_row(even, 1))
        pairs = [block for one in zip(evens, mates) for block in one]
        last_tiles = [(tile, 1) for tile in own] + [(tile, 1) for tile in pairs]
        links = [(tile, i) for i in (0, 2) for tile in pairs]
        link = functools.partial(link_kernel, R)
        sent, first = call_flat(link, [sent, other, side], links + last_tiles, [summed, (group, order)])
        turn = functools.partial(turn_kernel, R)
        sent, short = call_flat(turn, [sent, xor_col(sent, 1)], last_tiles + links, [summed, (group, rows)])
        (sent,) = call_flat(last_kernel, [first, short, sent, xor_col(sent, 1)], first_tiles, [(R // 2 * C,) + cut])
        whole = exchange(sent, ("chip", "col"))
        remaining, back = pl.pallas_call(
            functools.partial(closing_kernel, C),
            out_shape=(
                jax.ShapeDtypeStruct(solved.shape, F32),
                jax.ShapeDtypeStruct((2, nrhs, rows), F32),
            ),
            compiler_params=PARAMS,
        )(solved, factor_rows, whole, xor_row(whole, 1))
        return (back.transpose(0, 2, 1), remaining)

    return shards


def solution(mesh):
    R, C = mesh.shape["row"], mesh.shape["col"]

    def whole(factor_rows, solved, inverses, link_tile, right_side):
        group, size, rows = solved.shape[0] // R, inverses.shape[1] // R, inverses.shape[2] // C
        if group == 8 and size % 128 == 0 and rows % 256 == 0 and C == 4 and R % 2 == 0:
            split, row, build = Mesh(mesh.devices.reshape(R // 2, 2, C), ROW + ("col",)), ROW, tiled
        else:
            split, row, build = mesh, ("row",), generic
        both = row + ("col",)
        placed = (P(None, None, both), P(None, both), P(None, row, "col"), P("col", row), P(None, "col", None))
        return jax.shard_map(
            build(R, C),
            mesh=split,
            in_specs=placed,
            out_specs=(P(None, "col", None), P(None, both)),
            check_vma=False,
        )(factor_rows, solved, inverses, link_tile, right_side)

    return whole
```
